128 devices in a mesh: team: 8 (over y_lo, z), rep: 16 (over x, y_hi, core).
Axes of the slice: x: 4, y: 4 (y_hi: 2, y_lo: 2; y = y_hi * 2 + y_lo), z: 4, core: 2. Of those that a mesh axis runs over, the one named last changes fastest.
Arguments:
- affinity: bfloat16 [8, 256, 8, 128, 128], P('team', 'rep'), as said below
- col_index: int32 [8, 256, 8], P('team', 'rep'), may hold values from 0 to 31, all different within a row
- labels: int32 [32768], P(('rep', 'team')), may hold values from 0 to 511
Outputs:
- diffused: bfloat16 [32768, 512], P(('rep', 'team'))
The draws below stay inside these ranges and needn't reach their ends.
Inputs may be any that keep to these rules, and one draw needn't show every extreme that they name: `affinity`: every entry is positive. `col_index`: the 8 block columns of one block row are different.
All inputs are finite; a program needn't handle non-finite values.
Results may differ from the reference program's by a relative error of at most 0.017.
Values may be sent and summed in bfloat16 or wider, within the bound.
A program may use at most 128 MiB of HBM per device.

```python
import math
import jax
import jax.numpy as jnp
from jax import lax

C = 512
BLK = 128
KB = 8
ITERS = 3
ROWS_DEV = 256
NODES = 32768
NB = 256
COLB = 32
N_TEAM = 8
N_REP = 16


def draw_affinity(key, part):
    entries = KB * BLK * N_TEAM
    spread = math.sqrt(math.log(entries / 16.0))
    extent = (N_TEAM, NB, KB, BLK, BLK)
    normals = jax.random.normal(jax.random.fold_in(key, 11), extent, jnp.float32)
    normals = jnp.clip(normals, -4.5, 4.5)
    log_weight = spread * normals - 0.5 * spread * spread - math.log(entries)
    return jnp.exp(log_weight).astype(jnp.bfloat16)


def place_ends(values, own_key, low, high):
    shape = values.shape
    index_at = [jax.random.randint(jax.random.fold_in(own_key, axis), (), 0, shape[axis]) for axis in range(len(shape))]
    values = values.at[tuple(index_at)].set(low)
    longest = shape.index(max(shape))
    index_at[longest] = (index_at[longest] + 1) % shape[longest]
    return values.at[tuple(index_at)].set(high)


def different_ones(own_key, rows, amount, top, lift):
    ranking = jax.random.permutation(jax.random.fold_in(own_key, 1), amount)
    favour = ranking
    for power in range(3):
        favour = favour * favour // amount
    favour = favour * lift // amount
    chance = jax.random.randint(jax.random.fold_in(own_key, 2), (rows, amount), 0, 4096) + favour
    fixed_rows = jax.random.permutation(jax.random.fold_in(own_key, 3), rows)[jnp.arange(amount) % rows]
    chance = jnp.where(jnp.arange(rows)[:, None] == fixed_rows[None, :], 1 << 14, chance)
    score = chance * amount + jnp.arange(amount)
    return lax.top_k(score.astype(jnp.int32), top)[1].astype(jnp.int32)


def setup_inputs(seed: int = 0) -> dict:
    key_of = jax.random.split(jax.random.key(seed), 4)
    affinity = draw_affinity(jax.random.fold_in(key_of[3], 71), 0)
    col_index = different_ones(key_of[1], N_TEAM * NB, COLB, KB, 0).reshape((N_TEAM, NB, KB))
    labels = place_ends(jax.random.randint(key_of[2], (NODES,), 0, C), jax.random.fold_in(key_of[2], 1), 0, C - 1).astype(jnp.int32)
    return {"affinity": affinity, "col_index": col_index, "labels": labels}


def reference(affinity, col_index, labels):
    classes = jnp.arange(C, dtype=jnp.int32)
    seeded = (labels[:, None] == classes[None, :]).astype(jnp.float32) * 16.0
    current = seeded.astype(jnp.bfloat16)
    for step_index in range(ITERS):
        grouped = current.reshape(N_REP, N_TEAM, ROWS_DEV, C)
        summed_all = jnp.zeros((NODES, C), jnp.float32)
        for group in range(N_TEAM):
            column_rows = grouped[:, group].reshape(COLB, BLK, C).astype(jnp.float32)
            partials = jnp.zeros((NB, BLK, C), jnp.float32)
            for slot_index in range(KB):
                picked = column_rows[col_index[group, :, slot_index]]
                block_vals = affinity[group, :, slot_index].astype(jnp.float32)
                partials = partials + jnp.einsum('iab,ibc->iac', block_vals, picked)
            rounded = lax.optimization_barrier(partials.astype(jnp.bfloat16))
            summed_all = summed_all + rounded.astype(jnp.float32).reshape(NODES, C)
        blended = 0.9 * summed_all + 0.1 * seeded
        scale_rows = lax.rsqrt(lax.optimization_barrier(jnp.mean(blended * blended, axis=-1, keepdims=True)) + 1e-06)
        current = (blended * scale_rows).astype(jnp.bfloat16)
    return current
```

```python
import functools

import jax
import jax.numpy as jnp
from jax import lax
from jax.experimental import pallas as pl
from jax.experimental.pallas import tpu as pltpu
from jax.sharding import PartitionSpec as P

C = 512
BLK = 128
KB = 8
ITERS = 3
ROWS = 256
N_REP = 16
MESH = pl.DeviceIdType.MESH
F32 = jnp.float32
BF16 = jnp.bfloat16

CHUNKS = ((0, 64), (64, 64), (128, 64), (192, 64))
NQ = len(CHUNKS)

DZ2, DIR, COMB = 0, 1, 2
PARTNER, LEFT, RIGHT, LEFT_P, RIGHT_P, FAR, FAR_P, OWN = range(8)


def kernel(
    aff_hbm, col, lab, out,
    aff, lab_all, x0, x1, x2, p0, p1, p2, zin, yin, zout, yout,
    aff_sem, lab_send, lab_recv, z_send, z_recv, y_send, y_recv, g_send, g_recv, s_send, s_recv,
):
    r, t = lax.axis_index("rep"), lax.axis_index("team")
    x, yh, c = r // 4, (r // 2) % 2, r % 2
    yl, z = t // 4, t % 4

    def rep_of(dx=0, dyh=0, dc=0):
        return lax.rem(x + dx + 4, 4) * 4 + lax.rem(yh + dyh, 2) * 2 + lax.rem(c + dc, 2)

    def team_of(dz=0, dyl=0):
        return lax.rem(yl + dyl, 2) * 4 + lax.rem(z + dz + 4, 4)

    def z_of(dz):
        return lax.rem(z + dz + 4, 4)

    def remote(src, dst, send, recv, rep=None, team=None):
        return pltpu.make_async_remote_copy(
            src_ref=src, dst_ref=dst, send_sem=send, recv_sem=recv,
            device_id={"team": t if team is None else team, "rep": r if rep is None else rep},
            device_id_type=MESH,
        )

    xs, ps = (x0, x1, x2), (p0, p1, p2)
    started = []

    def go(copy):
        copy.start()
        started.append(copy)

    fetch = pltpu.make_async_copy(aff_hbm, aff, aff_sem)
    fetch.start()

    barrier = pltpu.get_barrier_semaphore()
    others = [lax.rem(r + k, N_REP) for k in range(1, N_REP)]
    for other in others:
        pl.semaphore_signal(barrier, inc=1, device_id={"team": t, "rep": other}, device_id_type=MESH)
    for other in (team_of(dz=1), team_of(dz=-1), team_of(dyl=1)):
        pl.semaphore_signal(barrier, inc=1, device_id={"team": other, "rep": r}, device_id_type=MESH)
    pl.semaphore_wait(barrier, N_REP - 1 + 3)

    lab_copies = []
    for k in range(1, N_REP):
        lab_copies.append(
            remote(lab, lab_all.at[r], lab_send.at[k - 1], lab_recv.at[k - 1], rep=lax.rem(r + k, N_REP))
        )
        lab_copies[-1].start()
    channel = lax.broadcasted_iota(jnp.int32, (BLK, C), 1)

    def seed(rep, rows_of):
        for h in range(2):
            x0[2 * rep + h] = jnp.where(rows_of(h)[:, None] == channel, 16.0, 0.0).astype(BF16)

    seed(r, lambda h: lab[h])
    for k in range(1, N_REP):
        lab_copies[k - 1].wait()
    def seed_one(k, carry):
        rep = lax.rem(r + k, N_REP)
        seed(rep, lambda h: lab_all[rep, h])
        return carry
    lax.fori_loop(1, N_REP, seed_one, 0)
    fetch.wait()

    for it in range(ITERS):
        cur, p = xs[it], ps[it]
        nxt = xs[it + 1] if it + 1 < ITERS else None

        def block_row(team, h, cur=cur, p=p):
            i = 2 * team + h
            acc = None
            for s in range(0, KB, 2):
                lhs = jnp.concatenate([aff[i, s], aff[i, s + 1]], axis=1)
                rhs = jnp.concatenate([cur[col[i, s]], cur[col[i, s + 1]]], axis=0)
                d = jnp.dot(lhs, rhs, preferred_element_type=F32)
                acc = d if acc is None else acc + d
            p[team, h * BLK : (h + 1) * BLK] = acc.astype(BF16)

        def pair(dz, h):
            block_row(z_of(dz), h)
            block_row(4 + z_of(dz), h)

        def products_far(h):
            pair(2, h)

        def products_near(h):
            def body(j, carry):
                pair(1 - j, h)
                return carry
            lax.fori_loop(0, 3, body, 0)

        def rows(q):
            return pl.ds(CHUNKS[q][0], CHUNKS[q][1])

        def z_copy(kind, v, q, dz, src, it=it):
            k = 2 * kind + v
            return remote(
                src, zin.at[it, k, rows(q)], z_send.at[it, q, k], z_recv.at[it, q, k], team=team_of(dz=dz)
            )

        def ahead(v):
            return 1 if v == 0 else -1

        def far(q):
            for v in range(2):
                go(z_copy(DZ2, v, q, ahead(v), p.at[4 * v + z_of(2), rows(q)]))

        def near(q):
            for v in range(2):
                go(z_copy(DIR, v, q, -ahead(v), p.at[4 * v + z_of(-ahead(v)), rows(q)]))

        def combine(q):
            for v in range(2):
                z_copy(DZ2, v, q, ahead(v), p.at[4 * v + z_of(2), rows(q)]).wait_recv()
                total = p[4 * v + z_of(ahead(v)), rows(q)].astype(F32) + zin[it, 2 * DZ2 + v, rows(q)].astype(F32)
                zout[it, v, rows(q)] = total.astype(BF16)
                go(z_copy(COMB, v, q, ahead(v), zout.at[it, v, rows(q)]))

        def z_sum(v, q):
            return (
                p[4 * v + z, rows(q)].astype(F32)
                + zin[it, 2 * DIR + v, rows(q)].astype(F32)
                + zin[it, 2 * COMB + v, rows(q)].astype(F32)
            )

        def y_copy(q):
            return remote(yout.at[it, rows(q)], yin.at[it, rows(q)], y_send.at[it, q], y_recv.at[it, q], team=team_of(dyl=1))

        def across(q):
            for v in range(2):
                z_copy(DIR, v, q, -ahead(v), p.at[0, rows(q)]).wait_recv()
                z_copy(COMB, v, q, ahead(v), zout.at[it, v, rows(q)]).wait_recv()
            yout[it, rows(q)] = z_sum(1 - yl, q).astype(BF16)
            go(y_copy(q))

        def place(rep, q):
            first, size = CHUNKS[q]
            return 2 * rep + first // BLK, pl.ds(first % BLK, size)

        def g_copy(kind, q, to, of):
            at = nxt.at[place(of, q)]
            return remote(at, at, g_send.at[it, q, kind], g_recv.at[it, q, kind], rep=to)

        def s_copy(kind, q, of):
            at = nxt.at[place(of, q)]
            return remote(at, at, s_send.at[it, q, kind], s_recv.at[it, q, kind], rep=rep_of(dc=1))

        left, right = rep_of(dx=-1), rep_of(dx=1)
        source = {
            OWN: r,
            PARTNER: rep_of(dyh=1),
            LEFT: left,
            RIGHT: right,
            LEFT_P: rep_of(dx=-1, dyh=1),
            RIGHT_P: rep_of(dx=1, dyh=1),
            FAR: rep_of(dx=2),
            FAR_P: rep_of(dx=2, dyh=1),
        }

        def got(kind, q):
            g_copy(kind, q, r, source[kind]).wait_recv()

        def share(kind, q):
            go(s_copy(kind, q, source[kind]))

        def finish(q):
            y_copy(q).wait_recv()
            seeded = x0[place(r, q)].astype(F32)
            blended = 0.9 * (z_sum(yl, q) + yin[it, rows(q)].astype(F32)) + 0.1 * seeded
            scale = lax.rsqrt(jnp.mean(blended * blended, axis=-1, keepdims=True) + 1e-6)
            scores = (blended * scale).astype(BF16)
            if nxt is None:
                out[rows(q)] = scores
                return
            nxt[place(r, q)] = scores
            go(g_copy(PARTNER, q, rep_of(dyh=1), r))
            go(g_copy(LEFT, q, right, r))
            go(g_copy(RIGHT, q, left, r))
            share(OWN, q)

        def spread_partner(q):
            got(PARTNER, q)
            go(g_copy(LEFT_P, q, right, source[PARTNER]))
            go(g_copy(RIGHT_P, q, left, source[PARTNER]))
            share(PARTNER, q)

        def spread_own(q):
            got(LEFT, q)
            go(g_copy(FAR, q, right, source[LEFT]))
            share(LEFT, q)
            got(RIGHT, q)
            share(RIGHT, q)

        def spread_last(q):
            got(RIGHT_P, q)
            go(g_copy(FAR_P, q, left, source[RIGHT_P]))
            share(RIGHT_P, q)
            got(LEFT_P, q)
            share(LEFT_P, q)

        def spread_far(q):
            for kind in (FAR, FAR_P):
                got(kind, q)
                share(kind, q)

        products_far(0)
        far(0)
        products_near(0)
        near(0)
        far(1)
        products_far(1)
        products_near(1)
        for k in range(1, NQ + 8):
            def do(step, q):
                if 0 <= q < NQ:
                    step(q)
            do(combine, k - 1)
            do(near, k)
            do(far, k + 1)
            do(across, k - 2)
            do(finish, k - 3)
            if nxt is not None:
                do(spread_partner, k - 4)
                do(spread_own, k - 4)
                do(spread_last, k - 5)
                do(spread_far, k - 6)
        if nxt is not None:
            for q in range(NQ):
                for kind in range(8):
                    g = {OWN: rep_of(dc=1)}.get(kind)
                    s_copy(kind, q, r).wait_recv()

    for copy in started:
        copy.wait_send()


def on_device(affinity, col_index, labels):
    vmem = pl.BlockSpec(memory_space=pltpu.VMEM)
    dma = pltpu.SemaphoreType.DMA
    scores = pltpu.VMEM((2 * N_REP, BLK, C), BF16)
    partials = pltpu.VMEM((8, ROWS, C), BF16)
    return pl.pallas_call(
        kernel,
        out_shape=jax.ShapeDtypeStruct((ROWS, C), BF16),
        in_specs=[pl.BlockSpec(memory_space=pl.ANY), pl.BlockSpec(memory_space=pltpu.SMEM), vmem],
        out_specs=vmem,
        scratch_shapes=[
            pltpu.VMEM((16, KB, BLK, BLK), BF16),
            pltpu.VMEM((N_REP, 2, BLK), jnp.int32),
            scores, scores, scores,
            partials, partials, partials,
            pltpu.VMEM((ITERS, 6, ROWS, C), BF16),
            pltpu.VMEM((ITERS, ROWS, C), BF16),
            pltpu.VMEM((ITERS, 2, ROWS, C), BF16),
            pltpu.VMEM((ITERS, ROWS, C), BF16),
            dma,
            dma((N_REP - 1,)), dma((N_REP - 1,)),
            dma((ITERS, NQ, 6)), dma((ITERS, NQ, 6)),
            dma((ITERS, NQ)), dma((ITERS, NQ)),
            dma((ITERS - 1, NQ, 7)), dma((ITERS - 1, NQ, 7)),
            dma((ITERS - 1, NQ, 8)), dma((ITERS - 1, NQ, 8)),
        ],
        compiler_params=pltpu.CompilerParams(
            collective_id=0, has_side_effects=True, vmem_limit_bytes=48 * 2**20
        ),
    )(affinity[0], col_index[0], labels.reshape(2, BLK))


def solution(mesh):
    in_specs = (P("team", "rep", None, None, None), P("team", "rep", None), P(("rep", "team")))
    out_specs = P(("rep", "team"), None)
    return jax.shard_map(
        on_device, mesh=mesh, in_specs=in_specs, out_specs=out_specs, check_vma=False
    )
```

```python
import functools

import jax
import jax.numpy as jnp
from jax import lax
from jax.experimental import pallas as pl
from jax.experimental.pallas import tpu as pltpu
from jax.sharding import PartitionSpec as P

C = 512
BLK = 128
KB = 8
ITERS = 3
ROWS = 256
N_REP = 16
MESH = pl.DeviceIdType.MESH
F32 = jnp.float32
BF16 = jnp.bfloat16

CHUNKS = (
    (0, 32, "Z", "P"),
    (32, 32, "Z", "P"),
    (64, 64, "Y", "X"),
    (128, 64, "Z", "P"),
    (192, 32, "Z", "P"),
    (224, 32, "Z", "D"),
)
ORDER = (
    ("m", 0), ("F", 0), ("m", 1), ("F", 1), ("F", 3), ("n", 0), ("o", 0), ("Y", 2), ("N", 0), ("C", 0), ("n", 1),
    ("N", 1), ("F", 4), ("C", 1), ("o", 1), ("N", 3), ("C", 3), ("A", 0), ("C", 4), ("A", 1), ("F", 5), ("E", 0),
    ("N", 4), ("W", 2), ("A", 3), ("C", 5), ("E", 1), ("N", 5), ("A", 4), ("L", 0), ("P", 0), ("C", 2), ("E", 3),
    ("A", 5), ("R", 0), ("P", 1), ("E", 4), ("E", 2), ("E", 5), ("R", 1), ("R", 2), ("P", 3), ("L", 2), ("L", 5),
    ("P", 2), ("P", 4), ("L", 1), ("M", 0), ("P", 5), ("L", 3), ("K", 1), ("M", 1), ("G", 2), ("R", 3), ("M", 3),
    ("L", 4), ("G", 5), ("K", 5), ("M", 4), ("R", 5), ("K", 0), ("R", 4), ("M", 5), ("G", 0), ("K", 3), ("H", 1),
    ("K", 4), ("M", 2), ("G", 1), ("H", 0), ("K", 2), ("H", 5), ("G", 3), ("H", 2), ("G", 4), ("H", 3), ("H", 4),
)
CHUNKS_LAST = (
    (0, 64, "Z", "P"),
    (64, 64, "Z", "P"),
    (128, 64, "Z", "P"),
    (192, 64, "Y", "P"),
)
ORDER_LAST = (
    ("m", 0), ("F", 0), ("n", 0), ("F", 1), ("m", 1), ("N", 1), ("n", 1), ("o", 1), ("F", 2), ("C", 0), ("Y", 3),
    ("C", 1), ("o", 0), ("N", 0), ("C", 2), ("N", 2), ("A", 1), ("W", 3), ("A", 0), ("A", 2), ("C", 3), ("E", 1),
    ("E", 0), ("E", 2), ("E", 3),
)
NQ = max(len(CHUNKS), len(CHUNKS_LAST))

DZ2, DIR, COMB = 0, 1, 2
PARTNER, LEFT, RIGHT, LEFT_P, RIGHT_P, FAR, FAR_P, OWN, FAR_2 = range(9)


def kernel(
    aff_hbm, col, lab, out,
    aff, lab_all, x0, x1, x2, p0, p1, p2, zin, yin, zout, yout, yall, ysum,
    aff_sem, lab_send, lab_recv, z_send, z_recv, y_send, y_recv, g_send, g_recv, s_send, s_recv,
):
    r, t = lax.axis_index("rep"), lax.axis_index("team")
    x, yh, c = r // 4, (r // 2) % 2, r % 2
    yl, z = t // 4, t % 4

    def rep_of(dx=0, dyh=0, dc=0):
        return lax.rem(x + dx + 4, 4) * 4 + lax.rem(yh + dyh, 2) * 2 + lax.rem(c + dc, 2)

    def team_of(dz=0, dyl=0):
        return lax.rem(yl + dyl, 2) * 4 + lax.rem(z + dz + 4, 4)

    def z_of(dz):
        return lax.rem(z + dz + 4, 4)

    def remote(src, dst, send, recv, rep=None, team=None):
        return pltpu.make_async_remote_copy(
            src_ref=src, dst_ref=dst, send_sem=send, recv_sem=recv,
            device_id={"team": t if team is None else team, "rep": r if rep is None else rep},
            device_id_type=MESH,
        )

    xs, ps = (x0, x1, x2), (p0, p1, p2)
    started = []

    def go(copy):
        copy.start()
        started.append(copy)

    fetch = pltpu.make_async_copy(aff_hbm, aff, aff_sem)
    fetch.start()

    barrier = pltpu.get_barrier_semaphore()
    others = [lax.rem(r + k, N_REP) for k in range(1, N_REP)]
    for other in others:
        pl.semaphore_signal(barrier, inc=1, device_id={"team": t, "rep": other}, device_id_type=MESH)
    for other in (team_of(dz=1), team_of(dz=-1), team_of(dyl=1)):
        pl.semaphore_signal(barrier, inc=1, device_id={"team": other, "rep": r}, device_id_type=MESH)
    pl.semaphore_wait(barrier, N_REP - 1 + 3)

    lab_copies = []
    for k in range(1, N_REP):
        lab_copies.append(
            remote(lab, lab_all.at[r], lab_send.at[k - 1], lab_recv.at[k - 1], rep=lax.rem(r + k, N_REP))
        )
        lab_copies[-1].start()
    channel = lax.broadcasted_iota(jnp.int32, (BLK, C), 1)

    def seed(rep, rows_of):
        for h in range(2):
            x0[2 * rep + h] = jnp.where(rows_of(h)[:, None] == channel, 16.0, 0.0).astype(BF16)

    seed(r, lambda h: lab[h])
    for k in range(1, N_REP):
        lab_copies[k - 1].wait()
    def seed_one(k, carry):
        rep = lax.rem(r + k, N_REP)
        seed(rep, lambda h: lab_all[rep, h])
        return carry
    lax.fori_loop(1, N_REP, seed_one, 0, unroll=3)
    fetch.wait()

    for it in range(ITERS):
        cur, p = xs[it], ps[it]
        nxt = xs[it + 1] if it + 1 < ITERS else None
        chunks, order = (CHUNKS, ORDER) if nxt is not None else (CHUNKS_LAST, ORDER_LAST)

        def block_row(team, h, cur=cur, p=p):
            i = 2 * team + h
            acc = None
            for s in range(0, KB, 2):
                lhs = jnp.concatenate([aff[i, s], aff[i, s + 1]], axis=1)
                rhs = jnp.concatenate([cur[col[s, i]], cur[col[s + 1, i]]], axis=0)
                d = jnp.dot(lhs, rhs, preferred_element_type=F32)
                acc = d if acc is None else acc + d
            p[team, h * BLK : (h + 1) * BLK] = acc.astype(BF16)

        def pair(dz, h):
            block_row(z_of(dz), h)
            block_row(4 + z_of(dz), h)

        def products_far(h):
            pair(2, h)

        def products_near(h):
            def body(j, carry):
                pair(1 - 2 * j, h)
                return carry
            lax.fori_loop(0, 2, body, 0)

        def products_here(h):
            pair(0, h)

        def rows(q):
            return pl.ds(chunks[q][0], chunks[q][1])

        def part(v, q):
            first, size, way, _ = chunks[q]
            return pl.ds(first, size) if way == "Z" else pl.ds(first + v * (size // 2), size // 2)

        def ahead(v):
            return 1 if v == 0 else -1

        def z_copy(kind, v, q, src):
            k = 2 * kind + v
            dz = -ahead(v) if kind == DIR else ahead(v)
            return remote(
                src, zin.at[it, k, part(v, q)], z_send.at[it, q, k], z_recv.at[it, q, k], team=team_of(dz=dz)
            )

        def term(v, dz, q):
            if chunks[q][2] == "Z":
                return p.at[4 * v + z_of(dz), part(v, q)]
            return ysum.at[it, z_of(dz), part(v, q)]

        def z_got(kind, v, q):
            z_copy(kind, v, q, zout.at[it, v, part(v, q)]).wait_recv()

        def far(q):
            for v in range(2):
                go(z_copy(DZ2, v, q, term(v, 2, q)))

        def near(q):
            for v in range(2):
                go(z_copy(DIR, v, q, term(v, -ahead(v), q)))

        def combine(q):
            for v in range(2):
                z_got(DZ2, v, q)
                total = term(v, ahead(v), q)[...].astype(F32) + zin[it, 2 * DZ2 + v, part(v, q)].astype(F32)
                zout[it, v, part(v, q)] = total.astype(BF16)
                go(z_copy(COMB, v, q, zout.at[it, v, part(v, q)]))

        def z_sum(v, q):
            return (
                term(v, 0, q)[...].astype(F32)
                + zin[it, 2 * DIR + v, part(v, q)].astype(F32)
                + zin[it, 2 * COMB + v, part(v, q)].astype(F32)
            )

        def y_copy(q):
            return remote(yout.at[it, rows(q)], yin.at[it, rows(q)], y_send.at[it, q], y_recv.at[it, q], team=team_of(dyl=1))

        def y_all_copy(q):
            return remote(
                p.at[pl.ds(4 * (1 - yl), 4), rows(q)], yall.at[it, :, rows(q)],
                y_send.at[it, q], y_recv.at[it, q], team=team_of(dyl=1),
            )

        def z_arrived(q):
            for v in range(2):
                z_got(DIR, v, q)
                z_got(COMB, v, q)

        def across(q):
            z_arrived(q)
            yout[it, rows(q)] = z_sum(1 - yl, q).astype(BF16)
            go(y_copy(q))

        def across_first(q):
            go(y_all_copy(q))

        def around(q):
            y_all_copy(q).wait_recv()
            for k in range(4):
                total = p[4 * yl + k, rows(q)].astype(F32) + yall[it, k, rows(q)].astype(F32)
                ysum[it, k, rows(q)] = total.astype(BF16)
            far(q)
            near(q)

        def place(rep, q, half=None):
            first, size = chunks[q][:2]
            if half is not None:
                first, size = first + half * (size // 2), size // 2
            return 2 * rep + first // BLK, pl.ds(first % BLK, size)

        left, right, partner = rep_of(dx=-1), rep_of(dx=1), rep_of(dyh=1)
        source = {
            OWN: r,
            PARTNER: partner,
            LEFT: left,
            RIGHT: right,
            LEFT_P: rep_of(dx=-1, dyh=1),
            RIGHT_P: rep_of(dx=1, dyh=1),
            FAR: rep_of(dx=2),
            FAR_P: rep_of(dx=2, dyh=1),
        }

        def g_copy(kind, q, to, of, half=None):
            at = nxt.at[place(of, q, half)]
            sem = FAR_2 if half == 1 else kind
            return remote(at, at, g_send.at[it, q, sem], g_recv.at[it, q, sem], rep=to)

        def s_copy(kind, q, of):
            at = nxt.at[place(of, q)]
            return remote(at, at, s_send.at[it, q, kind], s_recv.at[it, q, kind], rep=rep_of(dc=1))

        def finish(q):
            if chunks[q][2] == "Z":
                y_copy(q).wait_recv()
                sums = z_sum(yl, q) + yin[it, rows(q)].astype(F32)
            else:
                z_arrived(q)
                sums = jnp.concatenate([z_sum(0, q), z_sum(1, q)], axis=0)
            seeded = x0[place(r, q)].astype(F32)
            blended = 0.9 * sums + 0.1 * seeded
            scale = lax.rsqrt(jnp.mean(blended * blended, axis=-1, keepdims=True) + 1e-6)
            scores = (blended * scale).astype(BF16)
            if nxt is None:
                out[rows(q)] = scores
                return
            nxt[place(r, q)] = scores
            go(g_copy(PARTNER, q, partner, r))
            go(g_copy(LEFT, q, right, r))
            go(g_copy(RIGHT, q, left, r))
            if chunks[q][3] == "D":
                go(g_copy(LEFT_P, q, rep_of(dx=1, dyh=1), r))
                go(g_copy(RIGHT_P, q, rep_of(dx=-1, dyh=1), r))
                go(g_copy(FAR, q, rep_of(dx=2), r))
                go(g_copy(FAR_P, q, rep_of(dx=2, dyh=1), r))
            go(s_copy(OWN, q, r))

        def spread(kind, q):
            of, way = source[kind], chunks[q][3]
            halved = way == "X" and kind == FAR
            g_copy(kind, q, r, of, 0 if halved else None).wait_recv()
            if halved:
                g_copy(kind, q, r, of, 1).wait_recv()
            if way == "P":
                if kind == PARTNER:
                    go(g_copy(LEFT_P, q, right, of))
                    go(g_copy(RIGHT_P, q, left, of))
                if kind == LEFT:
                    go(g_copy(FAR, q, right, of))
                if kind == RIGHT_P:
                    go(g_copy(FAR_P, q, left, of))
            if way == "X":
                if kind == LEFT:
                    go(g_copy(FAR, q, right, of, 0))
                    go(g_copy(LEFT_P, q, partner, of))
                if kind == RIGHT:
                    go(g_copy(FAR, q, left, of, 1))
                    go(g_copy(RIGHT_P, q, partner, of))
                if kind == FAR:
                    go(g_copy(FAR_P, q, partner, of))
            go(s_copy(kind, q, of))

        steps = dict(
            m=products_far, n=products_near, o=products_here, F=far, N=near, C=combine, A=across,
            Y=across_first, W=around, E=finish,
            P=functools.partial(spread, PARTNER), L=functools.partial(spread, LEFT), R=functools.partial(spread, RIGHT),
            K=functools.partial(spread, LEFT_P), M=functools.partial(spread, RIGHT_P),
            G=functools.partial(spread, FAR), H=functools.partial(spread, FAR_P),
        )
        for step, q in order:
            steps[step](q)
        if nxt is not None:
            for q in range(len(chunks)):
                for kind in range(8):
                    s_copy(kind, q, r).wait_recv()

    for copy in started:
        copy.wait_send()


def on_device(affinity, col_index, labels):
    vmem = pl.BlockSpec(memory_space=pltpu.VMEM)
    dma = pltpu.SemaphoreType.DMA
    scores = pltpu.VMEM((2 * N_REP, BLK, C), BF16)
    partials = pltpu.VMEM((8, ROWS, C), BF16)
    return pl.pallas_call(
        kernel,
        out_shape=jax.ShapeDtypeStruct((ROWS, C), BF16),
        in_specs=[pl.BlockSpec(memory_space=pl.ANY), pl.BlockSpec(memory_space=pltpu.SMEM), vmem],
        out_specs=vmem,
        scratch_shapes=[
            pltpu.VMEM((16, KB, BLK, BLK), BF16),
            pltpu.VMEM((N_REP, 2, BLK), jnp.int32),
            scores, scores, scores,
            partials, partials, partials,
            pltpu.VMEM((ITERS, 6, ROWS, C), BF16),
            pltpu.VMEM((ITERS, ROWS, C), BF16),
            pltpu.VMEM((ITERS, 2, ROWS, C), BF16),
            pltpu.VMEM((ITERS, ROWS, C), BF16),
            pltpu.VMEM((ITERS, 4, ROWS, C), BF16),
            pltpu.VMEM((ITERS, 4, ROWS, C), BF16),
            dma,
            dma((N_REP - 1,)), dma((N_REP - 1,)),
            dma((ITERS, NQ, 6)), dma((ITERS, NQ, 6)),
            dma((ITERS, NQ)), dma((ITERS, NQ)),
            dma((ITERS - 1, NQ, 9)), dma((ITERS - 1, NQ, 9)),
            dma((ITERS - 1, NQ, 8)), dma((ITERS - 1, NQ, 8)),
        ],
        compiler_params=pltpu.CompilerParams(
            collective_id=0, has_side_effects=True, vmem_limit_bytes=60 * 2**20
        ),
    )(affinity[0], col_index[0].T, labels.reshape(2, BLK))


def solution(mesh):
    in_specs = (P("team", "rep", None, None, None), P("team", "rep", None), P(("rep", "team")))
    out_specs = P(("rep", "team"), None)
    return jax.shard_map(
        on_device, mesh=mesh, in_specs=in_specs, out_specs=out_specs, check_vma=False
    )
```

```python
import functools

import jax
import jax.numpy as jnp
from jax import lax
from jax.experimental import pallas as pl
from jax.experimental.pallas import tpu as pltpu
from jax.sharding import PartitionSpec as P

C = 512
BLK = 128
KB = 8
ITERS = 3
ROWS = 256
N_REP = 16
MESH = pl.DeviceIdType.MESH
F32 = jnp.float32
BF16 = jnp.bfloat16

CHUNKS = (
    (0, 64, "S", 2),
    (64, 64, "Z", 2),
    (128, 64, "Z", 2),
    (192, 64, "Y", 4),
)
ORDER = (
    ("m", 0), ("F", 0), ("n", 0), ("F", 1), ("m", 1), ("n", 1), ("o", 1), ("N", 0), ("Y", 3), ("C", 0), ("C", 1),
    ("o", 0), ("F", 2), ("A", 0), ("A", 1), ("W", 3), ("E", 0), ("C", 2), ("E", 1), ("C", 3), ("P", 0), ("L", 0),
    ("A", 2), ("P", 1), ("E", 3), ("M", 0), ("E", 2), ("M", 1), ("L", 1), ("P", 2), ("L", 2), ("P", 3), ("M", 2),
    ("S", 1), ("L", 3), ("M", 3), ("R", 3), ("S", 0), ("K", 3), ("S", 2), ("S", 3),
)
CHUNKS_LAST = (
    (0, 64, "S", 2),
    (64, 64, "Z", 2),
    (128, 64, "Z", 2),
    (192, 64, "Y", 2),
)
ORDER_LAST = (
    ("m", 0), ("F", 0), ("n", 0), ("F", 1), ("m", 1), ("n", 1), ("o", 1), ("F", 2), ("Y", 3), ("C", 1), ("N", 0),
    ("C", 2), ("o", 0), ("C", 0), ("A", 1), ("W", 3), ("A", 2), ("A", 0), ("C", 3), ("E", 1), ("E", 2), ("E", 0),
    ("E", 3),
)
NQ = max(len(CHUNKS), len(CHUNKS_LAST))

TERM = {(0, 2): 0, (1, 1): 1, (1, 3): 2, (1, 0): 3, (1, 2): 4, (0, 3): 5, (0, 1): 6, (0, 0): 7}
UP, DOWN, DIR_UP, DIR_DOWN, COMB_UP, COMB_DOWN = range(6)
PARTNER, LEFT, RIGHT, LEFT_P, RIGHT_P, FAR, FAR_P = range(7)
PLACE = {PARTNER: (0, 1), LEFT: (3, 0), RIGHT: (1, 0), LEFT_P: (3, 1), RIGHT_P: (1, 1), FAR: (2, 0), FAR_P: (2, 1)}


def kernel(
    aff_hbm, col, lab, out,
    aff, lab_all, x0, x1, x2, p0, p1, p2, zin, yin, zout, yout, yall, ysum,
    aff_sem, lab_send, lab_recv, z_send, z_recv, y_recv, g_send, g_recv, s_recv,
):
    r, t = lax.axis_index("rep"), lax.axis_index("team")
    x, yh, c = r // 4, (r // 2) % 2, r % 2
    yl, z = t // 4, t % 4

    def rep_of(dx=0, dyh=0, dc=0):
        return lax.rem(x + dx, 4) * 4 + lax.rem(yh + dyh, 2) * 2 + lax.rem(c + dc, 2)

    def team_of(dyl=0, dz=0):
        return lax.rem(yl + dyl, 2) * 4 + lax.rem(z + dz, 4)

    above, below, beside = team_of(dz=1), team_of(dz=3), team_of(dyl=1)
    right, left, partner, twin = rep_of(dx=1), rep_of(dx=3), rep_of(dyh=1), rep_of(dc=1)

    def remote(src, dst, send, recv, rep=None, team=None):
        return pltpu.make_async_remote_copy(
            src_ref=src, dst_ref=dst, send_sem=send, recv_sem=recv,
            device_id={"team": t if team is None else team, "rep": r if rep is None else rep},
            device_id_type=MESH,
        )

    xs, ps = (x0, x1, x2), (p0, p1, p2)

    fetch = pltpu.make_async_copy(aff_hbm, aff, aff_sem)
    fetch.start()

    barrier = pltpu.get_barrier_semaphore()
    others = [(dc, dx, dyh) for dc in range(2) for dx in range(4) for dyh in range(2)][1:]
    for dc, dx, dyh in others:
        pl.semaphore_signal(
            barrier, inc=1, device_id={"team": t, "rep": rep_of(dx, dyh, dc)}, device_id_type=MESH
        )
    for other in (above, below, beside):
        pl.semaphore_signal(barrier, inc=1, device_id={"team": other, "rep": r}, device_id_type=MESH)
    pl.semaphore_wait(barrier, N_REP - 1 + 3)

    lab_copies = []
    for k, (dc, dx, dyh) in enumerate(others):
        at = dc * 8 + (4 - dx) % 4 * 2 + dyh
        lab_copies.append(
            remote(lab, lab_all.at[at], lab_send, lab_recv.at[k], rep=rep_of(dx, dyh, dc))
        )
        lab_copies[-1].start()
    channel = lax.broadcasted_iota(jnp.int32, (BLK, C), 1)

    def seed(at, rows_of):
        for h in range(2):
            x0[at // 2, at % 2, h] = jnp.where(rows_of(h)[:, None] == channel, 16.0, 0.0).astype(BF16)

    seed(0, lambda h: lab[h])
    for copy in lab_copies:
        copy.wait_recv()

    def seed_one(at, carry):
        seed(at, lambda h: lab_all[at, h])
        return carry

    lax.fori_loop(1, N_REP, seed_one, 0, unroll=3)
    fetch.wait()

    for it in range(ITERS):
        cur, p = xs[it], ps[it]
        nxt = xs[it + 1] if it + 1 < ITERS else None
        chunks, order = (CHUNKS, ORDER) if nxt is not None else (CHUNKS_LAST, ORDER_LAST)

        def picked(i, s, cur=cur):
            block = col[s, i]
            owner = lax.div(block, 2)
            dx = lax.rem(lax.div(owner, 4) + 4 - x, 4)
            dyh = lax.rem(lax.rem(lax.div(owner, 2), 2) + yh, 2)
            dc = lax.rem(lax.rem(owner, 2) + c, 2)
            return cur[dc * 4 + dx, dyh, lax.rem(block, 2)]

        def block_row(w, dz, h, p=p, picked=picked):
            i = 2 * team_of(w, dz) + h
            acc = None
            for s in range(0, KB, 2):
                lhs = jnp.concatenate([aff[i, s], aff[i, s + 1]], axis=1)
                rhs = jnp.concatenate([picked(i, s), picked(i, s + 1)], axis=0)
                d = jnp.dot(lhs, rhs, preferred_element_type=F32)
                acc = d if acc is None else acc + d
            p[TERM[w, dz], h * BLK : (h + 1) * BLK] = acc.astype(BF16)

        def products_far(h):
            for w in range(2):
                block_row(w, 2, h)

        def products_near(h):
            for dz in (1, 3):
                for w in range(2):
                    block_row(w, dz, h)

        def products_here(h):
            for w in range(2):
                block_row(w, 0, h)

        def rows(q):
            return pl.ds(chunks[q][0], chunks[q][1])

        def half(w, q):
            first, size = chunks[q][:2]
            return pl.ds(first + w * (size // 2), size // 2)

        def z_copy(kind, q):
            way, size = chunks[q][2], rows(q)
            if kind in (COMB_UP, COMB_DOWN):
                at = kind - COMB_UP
                part = half(at, q) if way == "Y" else size
                src, dst = zout.at[it, at, part], zin.at[it, kind, part]
            elif way == "Y":
                dz, part, at = {
                    UP: (2, 0, 0), DIR_UP: (1, 1, 1), DOWN: (2, 1, 2), DIR_DOWN: (3, 0, 3)
                }[kind]
                part = half(part, q)
                src, dst = ysum.at[it, dz, part], zin.at[it, at, part]
            else:
                first, at = {UP: (0, 0), DIR_UP: (1, 1), DOWN: (4, 2), DIR_DOWN: (5, 3)}[kind]
                if way == "Z":
                    src, dst = p.at[pl.ds(first, 2), size], zin.at[it, pl.ds(at, 2), size]
                else:
                    src, dst = p.at[first, size], zin.at[it, at, size]
            to = above if kind in (UP, DIR_UP, COMB_UP) else below
            return remote(src, dst, z_send.at[it], z_recv.at[it, q, kind], team=to)

        def far(q):
            z_copy(UP, q).start()
            z_copy(DOWN, q).start()

        def near(q):
            z_copy(DIR_UP, q).start()
            z_copy(DIR_DOWN, q).start()

        def combine(q):
            for w in range(2):
                z_copy((UP, DOWN)[w], q).wait_recv()
                if chunks[q][2] == "Y":
                    part = half(w, q)
                    mine = ysum[it, (1, 3)[w], part]
                else:
                    part = rows(q)
                    mine = p[TERM[w, (1, 3)[w]], part]
                total = mine.astype(F32) + zin[it, 2 * w, part].astype(F32)
                zout[it, w, part] = total.astype(BF16)
                z_copy((COMB_UP, COMB_DOWN)[w], q).start()

        def z_arrived(q):
            for w in range(2):
                if chunks[q][2] != "Z":
                    z_copy((DIR_UP, DIR_DOWN)[w], q).wait_recv()
                z_copy((COMB_UP, COMB_DOWN)[w], q).wait_recv()

        def z_sum(w, q):
            if chunks[q][2] == "Y":
                part = half(w, q)
                mine = ysum[it, 0, part]
            else:
                part = rows(q)
                mine = p[TERM[w, 0], part]
            return mine.astype(F32) + zin[it, (3, 1)[w], part].astype(F32) + zin[it, 4 + w, part].astype(F32)

        def y_copy(q):
            if chunks[q][2] == "Y":
                src, dst = p.at[pl.ds(1, 4), rows(q)], yall.at[it, :, rows(q)]
            else:
                src, dst = yout.at[it, rows(q)], yin.at[it, rows(q)]
            return remote(src, dst, z_send.at[it], y_recv.at[it, q], team=beside)

        def across(q):
            z_arrived(q)
            yout[it, rows(q)] = z_sum(1, q).astype(BF16)
            y_copy(q).start()

        def across_first(q):
            y_copy(q).start()

        def around(q):
            y_copy(q).wait_recv()
            for k, dz in enumerate((1, 3, 0, 2)):
                total = p[TERM[0, dz], rows(q)].astype(F32) + yall[it, k, rows(q)].astype(F32)
                ysum[it, dz, rows(q)] = total.astype(BF16)
            far(q)
            near(q)

        def spot(q):
            first, size = chunks[q][:2]
            return first // BLK, pl.ds(first % BLK, size)

        def g_copy(kind, q, of, to):
            h, at = spot(q)
            (sx, sy), (dx, dy) = of, PLACE[kind]
            return remote(
                nxt.at[sx, sy, h, at], nxt.at[dx, dy, h, at], g_send.at[it], g_recv.at[it, q, kind], rep=to
            )

        def s_copy(k, q):
            h, at = spot(q)
            first, count = (((0, 1), (1, 3)) if chunks[q][3] == 2 else ((0, 1), (3, 1), (1, 1), (2, 1)))[k]
            return remote(
                nxt.at[pl.ds(first, count), :, h, at], nxt.at[pl.ds(4 + first, count), :, h, at],
                g_send.at[it], s_recv.at[it, q, k], rep=twin,
            )

        def finish(q):
            if chunks[q][2] == "Y":
                z_arrived(q)
                sums = jnp.concatenate([z_sum(0, q), z_sum(1, q)], axis=0)
            else:
                y_copy(q).wait_recv()
                sums = z_sum(0, q) + yin[it, rows(q)].astype(F32)
            h, at = spot(q)
            seeded = x0[0, 0, h, at].astype(F32)
            blended = 0.9 * sums + 0.1 * seeded
            scale = lax.rsqrt(jnp.mean(blended * blended, axis=-1, keepdims=True) + 1e-6)
            scores = (blended * scale).astype(BF16)
            if nxt is None:
                out[rows(q)] = scores
                return
            nxt[0, 0, h, at] = scores
            g_copy(PARTNER, q, (0, 0), partner).start()
            g_copy(LEFT, q, (0, 0), right).start()
            g_copy(RIGHT, q, (0, 0), left).start()

        def got(kind, q):
            g_copy(kind, q, (0, 0), partner).wait_recv()

        def spread_partner(q):
            got(PARTNER, q)
            g_copy(LEFT_P, q, (0, 1), right).start()
            g_copy(RIGHT_P, q, (0, 1), left).start()
            s_copy(0, q).start()

        def spread_left(q):
            got(LEFT, q)
            g_copy(FAR, q, (3, 0), right).start()

        def spread_right(q):
            got(RIGHT_P, q)
            g_copy(FAR_P, q, (1, 1), left).start()

        def share_left(q):
            got(LEFT_P, q)
            s_copy(1, q).start()

        def share_right(q):
            got(RIGHT, q)
            s_copy(2, q).start()

        def share_far(q):
            kinds = (LEFT_P, RIGHT, FAR, FAR_P) if chunks[q][3] == 2 else (FAR, FAR_P)
            for kind in kinds:
                got(kind, q)
            s_copy(chunks[q][3] - 1, q).start()

        steps = dict(
            m=products_far, n=products_near, o=products_here, F=far, N=near, C=combine, A=across,
            Y=across_first, W=around, E=finish, P=spread_partner, L=spread_left, M=spread_right,
            K=share_left, R=share_right, S=share_far,
        )
        for step, q in order:
            steps[step](q)
        if nxt is not None:
            for q in range(len(chunks)):
                for k in range(chunks[q][3]):
                    s_copy(k, q).wait_recv()

    remote(lab_all.at[pl.ds(1, N_REP - 1)], lab_all.at[pl.ds(1, N_REP - 1)], lab_send, lab_recv.at[0], rep=twin).wait_send()
    for it in range(ITERS):
        sent = ps[it].at[pl.ds(0, 7)]
        remote(sent, sent, z_send.at[it], y_recv.at[it, 0], team=beside).wait_send()
        if it + 1 < ITERS:
            sent = zin.at[:, pl.ds(0, 5)]
            remote(sent, sent, g_send.at[it], g_recv.at[it, 0, 0], rep=twin).wait_send()


def on_device(affinity, col_index, labels):
    vmem = pl.BlockSpec(memory_space=pltpu.VMEM)
    dma = pltpu.SemaphoreType.DMA
    scores = pltpu.VMEM((8, 2, 2, BLK, C), BF16)
    partials = pltpu.VMEM((8, ROWS, C), BF16)
    return pl.pallas_call(
        kernel,
        out_shape=jax.ShapeDtypeStruct((ROWS, C), BF16),
        in_specs=[pl.BlockSpec(memory_space=pl.ANY), pl.BlockSpec(memory_space=pltpu.SMEM), vmem],
        out_specs=vmem,
        scratch_shapes=[
            pltpu.VMEM((16, KB, BLK, BLK), BF16),
            pltpu.VMEM((N_REP, 2, BLK), jnp.int32),
            scores, scores, scores,
            partials, partials, partials,
            pltpu.VMEM((ITERS, 6, ROWS, C), BF16),
            pltpu.VMEM((ITERS, ROWS, C), BF16),
            pltpu.VMEM((ITERS, 2, ROWS, C), BF16),
            pltpu.VMEM((ITERS, ROWS, C), BF16),
            pltpu.VMEM((ITERS, 4, ROWS, C), BF16),
            pltpu.VMEM((ITERS, 4, ROWS, C), BF16),
            dma,
            dma, dma((N_REP - 1,)),
            dma((ITERS,)), dma((ITERS, NQ, 6)),
            dma((ITERS, NQ)),
            dma((ITERS - 1,)), dma((ITERS - 1, NQ, 7)),
            dma((ITERS - 1, NQ, 4)),
        ],
        compiler_params=pltpu.CompilerParams(
            collective_id=0, has_side_effects=True, vmem_limit_bytes=60 * 2**20
        ),
    )(affinity[0], col_index[0].T, labels.reshape(2, BLK))


def solution(mesh):
    in_specs = (P("team", "rep", None, None, None), P("team", "rep", None), P(("rep", "team")))
    out_specs = P(("rep", "team"), None)
    return jax.shard_map(
        on_device, mesh=mesh, in_specs=in_specs, out_specs=out_specs, check_vma=False
    )
```

```python
import functools

import jax
import jax.numpy as jnp
from jax import lax
from jax.experimental import pallas as pl
from jax.experimental.pallas import tpu as pltpu
from jax.sharding import PartitionSpec as P

C = 512
BLK = 128
KB = 8
ITERS = 3
ROWS = 256
N_REP = 16
MESH = pl.DeviceIdType.MESH
F32 = jnp.float32
BF16 = jnp.bfloat16

CHUNKS = (
    (0, 128, "S", 2, 0),
    (128, 128, "Z", 2, 0),
    (0, 128, "Z", 2, 1),
    (128, 128, "Z", 2, 1),
)
ORDER = (
    ("m", 0, 0), ("F", 0, 0), ("n", 0, 0), ("F", 0, 1), ("C", 0, 0), ("o", 0, 0), ("m", 0, 1), ("N", 0, 0),
    ("C", 0, 1), ("n", 0, 1), ("F", 0, 2), ("A", 0, 0), ("A", 0, 1), ("F", 0, 3), ("E", 0, 0), ("C", 0, 2),
    ("E", 0, 1), ("o", 0, 1), ("C", 0, 3), ("P", 0, 0), ("A", 0, 2), ("L", 0, 1), ("P", 0, 1), ("L", 0, 0),
    ("A", 0, 3), ("M", 0, 0), ("M", 0, 1), ("E", 0, 2), ("E", 0, 3), ("V", 0, 0), ("S", 0, 0), ("S", 0, 1),
    ("P", 0, 2), ("P", 0, 3), ("L", 0, 2), ("X", 0, 0), ("L", 0, 3), ("U", 0, 0), ("M", 0, 2), ("m", 1, 0),
    ("F", 1, 0), ("M", 0, 3), ("n", 1, 0), ("F", 1, 1), ("S", 0, 2), ("S", 0, 3), ("N", 1, 0), ("C", 1, 0),
    ("o", 1, 0), ("X", 0, 1), ("m", 1, 1), ("C", 1, 1), ("n", 1, 1), ("F", 1, 2), ("A", 1, 0), ("A", 1, 1),
    ("F", 1, 3), ("E", 1, 0), ("C", 1, 2), ("E", 1, 1), ("o", 1, 1), ("C", 1, 3), ("P", 1, 0), ("L", 1, 0),
    ("A", 1, 2), ("P", 1, 1), ("L", 1, 1), ("A", 1, 3), ("M", 1, 0), ("M", 1, 1), ("E", 1, 2), ("E", 1, 3),
    ("V", 1, 0), ("S", 1, 0), ("S", 1, 1), ("P", 1, 2), ("L", 1, 2), ("P", 1, 3), ("X", 1, 0), ("L", 1, 3),
    ("U", 1, 0), ("M", 1, 2), ("m", 2, 0), ("F", 2, 0), ("M", 1, 3), ("n", 2, 0), ("F", 2, 1), ("S", 1, 2),
    ("S", 1, 3), ("N", 2, 0), ("C", 2, 0), ("o", 2, 0), ("X", 1, 1), ("m", 2, 1), ("C", 2, 1), ("n", 2, 1),
    ("F", 2, 3), ("A", 2, 0), ("o", 2, 1), ("F", 2, 2), ("C", 2, 3), ("A", 2, 1), ("C", 2, 2), ("A", 2, 3),
    ("E", 2, 0), ("E", 2, 1), ("A", 2, 2), ("E", 2, 3), ("E", 2, 2), ("V", 2, 0),
)
NQ = len(CHUNKS)
HALF = C // 2

TERM = {(0, 2): 0, (1, 1): 1, (1, 3): 2, (1, 0): 3, (1, 2): 4, (0, 3): 5, (0, 1): 6, (0, 0): 7}
UP, DOWN, DIR_UP, DIR_DOWN, COMB_UP, COMB_DOWN = range(6)
PARTNER, LEFT, RIGHT, LEFT_P, RIGHT_P, FAR, FAR_P = range(7)
PLACE = {PARTNER: (0, 1), LEFT: (3, 0), RIGHT: (1, 0), LEFT_P: (3, 1), RIGHT_P: (1, 1), FAR: (2, 0), FAR_P: (2, 1)}


def kernel(
    aff_hbm, col, lab, out,
    aff, scaled, lab_all, x0a, x0b, x1a, x1b, x2a, x2b, p0, p1, p2, zin, yin, zout, yout, yall, ysum, squares, kept,
    scale0, scale1,
    aff_sem, lab_send, lab_recv, z_send, z_recv, y_recv, g_send, g_recv, s_recv, v_send, v_recv,
):
    r, t = lax.axis_index("rep"), lax.axis_index("team")
    x, yh, c = r // 4, (r // 2) % 2, r % 2
    yl, z = t // 4, t % 4

    def rep_of(dx=0, dyh=0, dc=0):
        return lax.rem(x + dx, 4) * 4 + lax.rem(yh + dyh, 2) * 2 + lax.rem(c + dc, 2)

    def team_of(dyl=0, dz=0):
        return lax.rem(yl + dyl, 2) * 4 + lax.rem(z + dz, 4)

    above, below, beside = team_of(dz=1), team_of(dz=3), team_of(dyl=1)
    right, left, partner, twin = rep_of(dx=1), rep_of(dx=3), rep_of(dyh=1), rep_of(dc=1)

    def remote(src, dst, send, recv, rep=None, team=None):
        return pltpu.make_async_remote_copy(
            src_ref=src, dst_ref=dst, send_sem=send, recv_sem=recv,
            device_id={"team": t if team is None else team, "rep": r if rep is None else rep},
            device_id_type=MESH,
        )

    xs, ps, scales = ((x0a, x0b), (x1a, x1b), (x2a, x2b)), (p0, p1, p2), (scale0, scale1)

    fetch = pltpu.make_async_copy(aff_hbm, aff, aff_sem)
    fetch.start()

    barrier = pltpu.get_barrier_semaphore()
    others = [(dc, dx, dyh) for dc in range(2) for dx in range(4) for dyh in range(2)][1:]
    others.sort(key=lambda o: -min(o[1], 4 - o[1]) - 2 * o[2])
    for dc, dx, dyh in others:
        pl.semaphore_signal(
            barrier, inc=1, device_id={"team": t, "rep": rep_of(dx, dyh, dc)}, device_id_type=MESH
        )
    for other in (above, below, beside):
        pl.semaphore_signal(barrier, inc=1, device_id={"team": other, "rep": r}, device_id_type=MESH)
    pl.semaphore_wait(barrier, N_REP - 1 + 3)

    lab_copies = []
    for k, (dc, dx, dyh) in enumerate(others):
        at = dc * 8 + (4 - dx) % 4 * 2 + dyh
        lab_copies.append(
            remote(lab, lab_all.at[at], lab_send, lab_recv.at[k], rep=rep_of(dx, dyh, dc))
        )
        lab_copies[-1].start()
    channel = lax.broadcasted_iota(jnp.int32, (BLK, HALF), 1)

    def seed(at, rows_of):
        for h in range(2):
            label = rows_of(h)[:, None]
            for n in range(2):
                x0 = xs[0][n]
                x0[at // 2, at % 2, h] = jnp.where(label == channel + n * HALF, 16.0, 0.0).astype(BF16)

    seed(0, lambda h: lab[h])
    for copy in lab_copies:
        copy.wait_recv()

    def seed_one(at, carry):
        seed(at, lambda h: lab_all[at, h])
        return carry

    lax.fori_loop(1, N_REP, seed_one, 0, unroll=3)
    fetch.wait()

    def steps_of(it):
        p = ps[it]
        nxt = xs[it + 1] if it + 1 < ITERS else None
        chunks = CHUNKS

        def place_of(i, s):
            block = col[s, i]
            owner = lax.div(block, 2)
            dx = lax.rem(lax.div(owner, 4) + 4 - x, 4)
            dyh = lax.rem(lax.rem(lax.div(owner, 2), 2) + yh, 2)
            dc = lax.rem(lax.rem(owner, 2) + c, 2)
            return dc * 4 + dx, dyh, lax.rem(block, 2)

        def block_row(w, dz, h, n):
            i = 2 * team_of(w, dz) + h
            cur = xs[it][n]
            places = [place_of(i, s) for s in range(KB)]

            def weights(s):
                if it == 0:
                    return aff[i, s]
                if n == 1:
                    return scaled[TERM[w, dz], h, s]
                a, b, k = places[s]
                by = scales[it - 1][2 * a + b, pl.ds(k, 1)]
                product = (aff[i, s].astype(F32) * by).astype(BF16)
                scaled[TERM[w, dz], h, s] = product
                return product

            acc = None
            for s in range(0, KB, 2):
                lhs = jnp.concatenate([weights(s), weights(s + 1)], axis=1)
                rhs = jnp.concatenate([cur[places[s]], cur[places[s + 1]]], axis=0)
                d = jnp.dot(lhs, rhs, preferred_element_type=F32)
                acc = d if acc is None else acc + d
            p[n, TERM[w, dz], h * BLK : (h + 1) * BLK] = acc.astype(BF16)

        def products(dzs, n):
            for dz in dzs:
                for h in range(2):
                    for w in range(2):
                        block_row(w, dz, h, n)

        def n_of(q):
            return chunks[q][4]

        def rows(q):
            return pl.ds(chunks[q][0], chunks[q][1])

        def half(w, q):
            first, size = chunks[q][:2]
            return pl.ds(first + w * (size // 2), size // 2)

        def z_copy(kind, q):
            way, size, n = chunks[q][2], rows(q), n_of(q)
            if kind in (COMB_UP, COMB_DOWN):
                at = kind - COMB_UP
                part = half(at, q) if way == "Y" else size
                src, dst = zout.at[it, n, at, part], zin.at[it, n, kind, part]
            elif way == "Y":
                dz, part, at = {
                    UP: (2, 0, 0), DIR_UP: (1, 1, 1), DOWN: (2, 1, 2), DIR_DOWN: (3, 0, 3)
                }[kind]
                part = half(part, q)
                src, dst = ysum.at[it, n, dz, part], zin.at[it, n, at, part]
            else:
                first, at = {UP: (0, 0), DIR_UP: (1, 1), DOWN: (4, 2), DIR_DOWN: (5, 3)}[kind]
                if way == "Z":
                    src, dst = p.at[n, pl.ds(first, 2), size], zin.at[it, n, pl.ds(at, 2), size]
                else:
                    src, dst = p.at[n, first, size], zin.at[it, n, at, size]
            to = above if kind in (UP, DIR_UP, COMB_UP) else below
            return remote(src, dst, z_send.at[it], z_recv.at[it, q, kind], team=to)

        def far(q):
            z_copy(UP, q).start()
            z_copy(DOWN, q).start()

        def near(q):
            z_copy(DIR_UP, q).start()
            z_copy(DIR_DOWN, q).start()

        def combine(q):
            for w in range(2):
                z_copy((UP, DOWN)[w], q).wait_recv()
                if chunks[q][2] == "Y":
                    part = half(w, q)
                    mine = ysum[it, n_of(q), (1, 3)[w], part]
                else:
                    part = rows(q)
                    mine = p[n_of(q), TERM[w, (1, 3)[w]], part]
                total = mine.astype(F32) + zin[it, n_of(q), 2 * w, part].astype(F32)
                zout[it, n_of(q), w, part] = total.astype(BF16)
                z_copy((COMB_UP, COMB_DOWN)[w], q).start()

        def z_arrived(q):
            for w in range(2):
                if chunks[q][2] != "Z":
                    z_copy((DIR_UP, DIR_DOWN)[w], q).wait_recv()
                z_copy((COMB_UP, COMB_DOWN)[w], q).wait_recv()

        def z_sum(w, q):
            if chunks[q][2] == "Y":
                part = half(w, q)
                mine = ysum[it, n_of(q), 0, part]
            else:
                part = rows(q)
                mine = p[n_of(q), TERM[w, 0], part]
            arrived = [zin[it, n_of(q), k, part].astype(F32) for k in ((3, 1)[w], 4 + w)]
            return mine.astype(F32) + arrived[0] + arrived[1]

        def y_copy(q):
            if chunks[q][2] == "Y":
                src, dst = p.at[n_of(q), pl.ds(1, 4), rows(q)], yall.at[it, n_of(q), :, rows(q)]
            else:
                src, dst = yout.at[it, n_of(q), rows(q)], yin.at[it, n_of(q), rows(q)]
            return remote(src, dst, z_send.at[it], y_recv.at[it, q], team=beside)

        def across(q):
            z_arrived(q)
            yout[it, n_of(q), rows(q)] = z_sum(1, q).astype(BF16)
            y_copy(q).start()

        def across_first(q):
            y_copy(q).start()

        def around(q):
            y_copy(q).wait_recv()
            for k, dz in enumerate((1, 3, 0, 2)):
                total = p[n_of(q), TERM[0, dz], rows(q)].astype(F32) + yall[it, n_of(q), k, rows(q)].astype(F32)
                ysum[it, n_of(q), dz, rows(q)] = total.astype(BF16)
            far(q)
            near(q)

        def spot(q):
            first, size = chunks[q][:2]
            return first // BLK, pl.ds(first % BLK, size)

        def g_copy(kind, q, of, to):
            h, at = spot(q)
            (sx, sy), (dx, dy) = of, PLACE[kind]
            return remote(
                nxt[n_of(q)].at[sx, sy, h, at], nxt[n_of(q)].at[dx, dy, h, at], g_send.at[it], g_recv.at[it, q, kind], rep=to
            )

        def s_copy(k, q):
            h, at = spot(q)
            first, count = (((0, 1), (1, 3)) if chunks[q][3] == 2 else ((0, 1), (3, 1), (1, 1), (2, 1)))[k]
            return remote(
                nxt[n_of(q)].at[pl.ds(first, count), :, h, at], nxt[n_of(q)].at[pl.ds(4 + first, count), :, h, at],
                g_send.at[it], s_recv.at[it, q, k], rep=twin,
            )

        def finish(q):
            if chunks[q][2] == "Y":
                z_arrived(q)
                sums = jnp.concatenate([z_sum(0, q), z_sum(1, q)], axis=0)
            else:
                y_copy(q).wait_recv()
                sums = z_sum(0, q) + yin[it, n_of(q), rows(q)].astype(F32)
            h, at = spot(q)
            seeded = xs[0][n_of(q)][0, 0, h, at].astype(F32)
            blended = 0.9 * sums + 0.1 * seeded
            left_half, right_half = blended[:, : HALF // 2], blended[:, HALF // 2 :]
            squares[n_of(q), rows(q)] = left_half * left_half + right_half * right_half
            if nxt is None:
                kept[n_of(q), rows(q)] = blended
                return
            nxt[n_of(q)][0, 0, h, at] = blended.astype(BF16)
            g_copy(PARTNER, q, (0, 0), partner).start()
            g_copy(LEFT, q, (0, 0), right).start()
            g_copy(RIGHT, q, (0, 0), left).start()

        def got(kind, q):
            g_copy(kind, q, (0, 0), partner).wait_recv()

        def spread_partner(q):
            got(PARTNER, q)
            g_copy(LEFT_P, q, (0, 1), right).start()
            g_copy(RIGHT_P, q, (0, 1), left).start()
            s_copy(0, q).start()

        def spread_left(q):
            got(LEFT, q)
            g_copy(FAR, q, (3, 0), right).start()

        def spread_right(q):
            got(RIGHT_P, q)
            g_copy(FAR_P, q, (1, 1), left).start()

        def share_left(q):
            got(LEFT_P, q)
            s_copy(1, q).start()

        def share_right(q):
            got(RIGHT, q)
            s_copy(2, q).start()

        def share_far(q):
            kinds = (LEFT_P, RIGHT, FAR, FAR_P) if chunks[q][3] == 2 else (FAR, FAR_P)
            for kind in kinds:
                got(kind, q)
            s_copy(chunks[q][3] - 1, q).start()

        def v_copy(k):
            dc, dx, dyh = others[k]
            at = dc * 8 + (4 - dx) % 4 * 2 + dyh
            own = scales[it].at[0]
            return remote(own, scales[it].at[at], v_send.at[it], v_recv.at[it, k], rep=rep_of(dx, dyh, dc))

        def send_scales(_):
            diagonal = lax.broadcasted_iota(jnp.int32, (BLK, BLK), 0) == lax.broadcasted_iota(jnp.int32, (BLK, BLK), 1)
            for h in range(2):
                at = pl.ds(h * BLK, BLK)
                mean = jnp.sum(squares[0, at] + squares[1, at], axis=-1, keepdims=True) / C
                scale = lax.rsqrt(mean + 1e-6)
                if nxt is None:
                    for n in range(2):
                        out[at, n * HALF : (n + 1) * HALF] = (kept[n, at] * scale).astype(BF16)
                else:
                    scales[it][0, pl.ds(h, 1)] = jnp.sum(jnp.where(diagonal, scale, 0.0), axis=0, keepdims=True)
            if nxt is not None:
                for k in range(N_REP - 1):
                    v_copy(k).start()

        def take_scales(_):
            for k in range(N_REP - 1):
                v_copy(k).wait_recv()

        def take_shares(n):
            for q in range(NQ):
                if n_of(q) == n:
                    for k in range(chunks[q][3]):
                        s_copy(k, q).wait_recv()

        return dict(
            m=functools.partial(products, (2,)), n=functools.partial(products, (1, 3)), o=functools.partial(products, (0,)),
            F=far, N=near, C=combine, A=across, Y=across_first, W=around, E=finish,
            P=spread_partner, L=spread_left, M=spread_right, K=share_left, R=share_right, S=share_far,
            V=send_scales, U=take_scales, X=take_shares,
        )

    steps = [steps_of(it) for it in range(ITERS)]
    for step, it, q in ORDER:
        steps[it][step](q)

    remote(lab_all.at[pl.ds(1, N_REP - 1)], lab_all.at[pl.ds(1, N_REP - 1)], lab_send, lab_recv.at[0], rep=twin).wait_send()
    for it in range(ITERS):
        sent = ps[it].at[:, pl.ds(0, 7)]
        remote(sent, sent, z_send.at[it], y_recv.at[it, 0], team=beside).wait_send()
        if it + 1 < ITERS:
            sent = zin.at[:, :, pl.ds(0, 5)]
            remote(sent, sent, g_send.at[it], g_recv.at[it, 0, 0], rep=twin).wait_send()
            sent = scales[it].at[pl.ds(1, N_REP - 1)]
            remote(sent, sent, v_send.at[it], v_recv.at[it, 0], rep=twin).wait_send()


def on_device(affinity, col_index, labels):
    vmem = pl.BlockSpec(memory_space=pltpu.VMEM)
    dma = pltpu.SemaphoreType.DMA
    scores = pltpu.VMEM((8, 2, 2, BLK, HALF), BF16)
    partials = pltpu.VMEM((2, 8, ROWS, HALF), BF16)
    return pl.pallas_call(
        kernel,
        out_shape=jax.ShapeDtypeStruct((ROWS, C), BF16),
        in_specs=[pl.BlockSpec(memory_space=pl.ANY), pl.BlockSpec(memory_space=pltpu.SMEM), vmem],
        out_specs=vmem,
        scratch_shapes=[
            pltpu.VMEM((16, KB, BLK, BLK), BF16),
            pltpu.VMEM((8, 2, KB, BLK, BLK), BF16),
            pltpu.VMEM((N_REP, 2, BLK), jnp.int32),
            scores, scores, scores, scores, scores, scores,
            partials, partials, partials,
            pltpu.VMEM((ITERS, 2, 6, ROWS, HALF), BF16),
            pltpu.VMEM((ITERS, 2, ROWS, HALF), BF16),
            pltpu.VMEM((ITERS, 2, 2, ROWS, HALF), BF16),
            pltpu.VMEM((ITERS, 2, ROWS, HALF), BF16),
            pltpu.VMEM((ITERS, 2, 4, ROWS, HALF), BF16),
            pltpu.VMEM((ITERS, 2, 4, ROWS, HALF), BF16),
            pltpu.VMEM((2, ROWS, HALF // 2), F32),
            pltpu.VMEM((2, ROWS, HALF), F32),
            pltpu.VMEM((N_REP, 2, BLK), F32), pltpu.VMEM((N_REP, 2, BLK), F32),
            dma,
            dma, dma((N_REP - 1,)),
            dma((ITERS,)), dma((ITERS, NQ, 6)),
            dma((ITERS, NQ)),
            dma((ITERS - 1,)), dma((ITERS - 1, NQ, 7)),
            dma((ITERS - 1, NQ, 4)),
            dma((ITERS - 1,)), dma((ITERS - 1, N_REP - 1)),
        ],
        compiler_params=pltpu.CompilerParams(
            collective_id=0, has_side_effects=True, vmem_limit_bytes=60 * 2**20
        ),
    )(affinity[0], col_index[0].T, labels.reshape(2, BLK))


def solution(mesh):
    in_specs = (P("team", "rep", None, None, None), P("team", "rep", None), P(("rep", "team")))
    out_specs = P(("rep", "team"), None)
    return jax.shard_map(
        on_device, mesh=mesh, in_specs=in_specs, out_specs=out_specs, check_vma=False
    )
```

```python
import functools

import jax
import jax.numpy as jnp
from jax import lax
from jax.experimental import pallas as pl
from jax.experimental.pallas import tpu as pltpu
from jax.sharding import PartitionSpec as P

C = 512
BLK = 128
KB = 8
ITERS = 3
ROWS = 256
N_REP = 16
MESH = pl.DeviceIdType.MESH
F32 = jnp.float32
BF16 = jnp.bfloat16

CHUNKS = (
    ((0, 128, "S", 2, 0), (128, 128, "S", 2, 0), (0, 128, "S", 2, 1), (128, 128, "S", 2, 1),),
    ((0, 128, "S", 2, 0), (128, 128, "S", 2, 0), (0, 128, "S", 2, 1), (128, 128, "S", 2, 1),),
    ((0, 128, "S", 2, 0), (128, 128, "Z", 2, 0), (0, 128, "Y", 2, 1), (128, 128, "Z", 2, 1),),
)
ORDER = (
    ("m", 0, 0), ("F", 0, 0), ("n", 0, 0), ("F", 0, 1), ("N", 0, 0), ("o", 0, 0), ("m", 0, 1), ("N", 0, 1),
    ("C", 0, 0), ("C", 0, 1), ("n", 0, 1), ("F", 0, 2), ("A", 0, 0), ("N", 0, 2), ("F", 0, 3), ("A", 0, 1),
    ("N", 0, 3), ("E", 0, 0), ("C", 0, 2), ("E", 0, 1), ("o", 0, 1), ("C", 0, 3), ("P", 0, 0), ("A", 0, 2),
    ("P", 0, 1), ("L", 0, 1), ("L", 0, 0), ("A", 0, 3), ("M", 0, 0), ("M", 0, 1), ("E", 0, 2), ("E", 0, 3),
    ("V", 0, 0), ("S", 0, 0), ("S", 0, 1), ("P", 0, 2), ("P", 0, 3), ("L", 0, 2), ("L", 0, 3), ("X", 0, 0),
    ("U", 0, 0), ("m", 1, 0), ("F", 1, 0), ("M", 0, 2), ("n", 1, 0), ("F", 1, 1), ("M", 0, 3), ("N", 1, 0),
    ("C", 1, 0), ("S", 0, 2), ("S", 0, 3), ("N", 1, 1), ("C", 1, 1), ("o", 1, 0), ("X", 0, 1), ("m", 1, 1),
    ("F", 1, 2), ("A", 1, 0), ("F", 1, 3), ("n", 1, 1), ("N", 1, 3), ("A", 1, 1), ("N", 1, 2), ("E", 1, 0),
    ("C", 1, 2), ("o", 1, 1), ("E", 1, 1), ("C", 1, 3), ("L", 1, 0), ("P", 1, 0), ("A", 1, 2), ("P", 1, 1),
    ("A", 1, 3), ("L", 1, 1), ("M", 1, 0), ("E", 1, 2), ("M", 1, 1), ("E", 1, 3), ("V", 1, 0), ("P", 1, 2),
    ("S", 1, 0), ("L", 1, 3), ("L", 1, 2), ("P", 1, 3), ("S", 1, 1), ("U", 1, 0), ("M", 1, 2), ("X", 1, 0),
    ("M", 1, 3), ("m", 2, 0), ("F", 2, 0), ("n", 2, 0), ("S", 1, 2), ("N", 2, 0), ("S", 1, 3), ("o", 2, 0),
    ("F", 2, 1), ("C", 2, 0), ("X", 1, 1), ("m", 2, 1), ("n", 2, 1), ("o", 2, 1), ("Y", 2, 2), ("F", 2, 3),
    ("C", 2, 1), ("C", 2, 3), ("A", 2, 0), ("A", 2, 1), ("W", 2, 2), ("A", 2, 3), ("C", 2, 2), ("E", 2, 0),
    ("E", 2, 1), ("E", 2, 3), ("E", 2, 2), ("V", 2, 0),
)
NQ = len(CHUNKS[0])
HALF = C // 2

TERM = {(0, 2): 0, (1, 1): 1, (1, 3): 2, (1, 0): 3, (1, 2): 4, (0, 3): 5, (0, 1): 6, (0, 0): 7}
UP, DOWN, DIR_UP, DIR_DOWN, COMB_UP, COMB_DOWN = range(6)
PARTNER, LEFT, RIGHT, LEFT_P, RIGHT_P, FAR, FAR_P = range(7)
PLACE = {PARTNER: (0, 1), LEFT: (3, 0), RIGHT: (1, 0), LEFT_P: (3, 1), RIGHT_P: (1, 1), FAR: (2, 0), FAR_P: (2, 1)}


def kernel(
    aff_hbm, col, lab, out,
    aff, scaled, lab_all, x0a, x0b, x1a, x1b, x2a, x2b, p0, p1, p2, zin, yin, zout, yout, yall, ysum, squares, kept,
    scale0, scale1,
    aff_sem, lab_send, lab_recv, z_send, z_recv, y_recv, g_send, g_recv, s_recv, v_send, v_recv,
):
    r, t = lax.axis_index("rep"), lax.axis_index("team")
    x, yh, c = r // 4, (r // 2) % 2, r % 2
    yl, z = t // 4, t % 4

    def rep_of(dx=0, dyh=0, dc=0):
        return lax.rem(x + dx, 4) * 4 + lax.rem(yh + dyh, 2) * 2 + lax.rem(c + dc, 2)

    def team_of(dyl=0, dz=0):
        return lax.rem(yl + dyl, 2) * 4 + lax.rem(z + dz, 4)

    above, below, beside = team_of(dz=1), team_of(dz=3), team_of(dyl=1)
    right, left, partner, twin = rep_of(dx=1), rep_of(dx=3), rep_of(dyh=1), rep_of(dc=1)

    def remote(src, dst, send, recv, rep=None, team=None):
        return pltpu.make_async_remote_copy(
            src_ref=src, dst_ref=dst, send_sem=send, recv_sem=recv,
            device_id={"team": t if team is None else team, "rep": r if rep is None else rep},
            device_id_type=MESH,
        )

    xs, ps, scales = ((x0a, x0b), (x1a, x1b), (x2a, x2b)), (p0, p1, p2), (scale0, scale1)

    fetch = pltpu.make_async_copy(aff_hbm, aff, aff_sem)
    fetch.start()

    barrier = pltpu.get_barrier_semaphore()
    others = [(dc, dx, dyh) for dc in range(2) for dx in range(4) for dyh in range(2)][1:]
    others.sort(key=lambda o: -min(o[1], 4 - o[1]) - 2 * o[2])
    for dc, dx, dyh in others:
        pl.semaphore_signal(
            barrier, inc=1, device_id={"team": t, "rep": rep_of(dx, dyh, dc)}, device_id_type=MESH
        )
    for other in (above, below, beside):
        pl.semaphore_signal(barrier, inc=1, device_id={"team": other, "rep": r}, device_id_type=MESH)
    pl.semaphore_wait(barrier, N_REP - 1 + 3)

    lab_copies = []
    for k, (dc, dx, dyh) in enumerate(others):
        at = dc * 8 + (4 - dx) % 4 * 2 + dyh
        lab_copies.append(
            remote(lab, lab_all.at[at], lab_send, lab_recv.at[k], rep=rep_of(dx, dyh, dc))
        )
        lab_copies[-1].start()
    channel = lax.broadcasted_iota(jnp.int32, (BLK, HALF), 1)

    def seed(at, rows_of):
        for h in range(2):
            label = rows_of(h)[:, None]
            for n in range(2):
                x0 = xs[0][n]
                x0[at // 2, at % 2, h] = jnp.where(label == channel + n * HALF, 16.0, 0.0).astype(BF16)

    seed(0, lambda h: lab[h])
    for k in reversed(range(N_REP - 1)):
        dc, dx, dyh = others[k]
        at = dc * 8 + (4 - dx) % 4 * 2 + dyh
        lab_copies[k].wait_recv()
        seed(at, lambda h, at=at: lab_all[at, h])
    fetch.wait()

    def steps_of(it):
        p = ps[it]
        nxt = xs[it + 1] if it + 1 < ITERS else None
        chunks = CHUNKS[it]

        def place_of(i, s):
            block = col[s, i]
            owner = lax.div(block, 2)
            dx = lax.rem(lax.div(owner, 4) + 4 - x, 4)
            dyh = lax.rem(lax.rem(lax.div(owner, 2), 2) + yh, 2)
            dc = lax.rem(lax.rem(owner, 2) + c, 2)
            return dc * 4 + dx, dyh, lax.rem(block, 2)

        def block_row(w, dz, h, n):
            i = 2 * team_of(w, dz) + h
            cur = xs[it][n]
            places = [place_of(i, s) for s in range(KB)]

            def weights(s):
                if it == 0:
                    return aff[i, s]
                if n == 1:
                    return scaled[TERM[w, dz], h, s]
                a, b, k = places[s]
                by = scales[it - 1][2 * a + b, pl.ds(k, 1)]
                product = (aff[i, s].astype(F32) * by).astype(BF16)
                scaled[TERM[w, dz], h, s] = product
                return product

            acc = None
            for s in range(0, KB, 2):
                lhs = jnp.concatenate([weights(s), weights(s + 1)], axis=1)
                rhs = jnp.concatenate([cur[places[s]], cur[places[s + 1]]], axis=0)
                d = jnp.dot(lhs, rhs, preferred_element_type=F32)
                acc = d if acc is None else acc + d
            p[n, TERM[w, dz], h * BLK : (h + 1) * BLK] = acc.astype(BF16)

        def products(dzs, n):
            for dz in dzs:
                for h in range(2):
                    for w in range(2):
                        block_row(w, dz, h, n)

        def n_of(q):
            return chunks[q][4]

        def rows(q):
            return pl.ds(chunks[q][0], chunks[q][1])

        def half(w, q):
            first, size = chunks[q][:2]
            return pl.ds(first + w * (size // 2), size // 2)

        def z_copy(kind, q):
            way, size, n = chunks[q][2], rows(q), n_of(q)
            if kind in (COMB_UP, COMB_DOWN):
                at = kind - COMB_UP
                part = half(at, q) if way == "Y" else size
                src, dst = zout.at[it, n, at, part], zin.at[it, n, kind, part]
            elif way == "Y":
                dz, part, at = {
                    UP: (2, 0, 0), DIR_UP: (1, 1, 1), DOWN: (2, 1, 2), DIR_DOWN: (3, 0, 3)
                }[kind]
                part = half(part, q)
                src, dst = ysum.at[it, n, dz, part], zin.at[it, n, at, part]
            else:
                first, at = {UP: (0, 0), DIR_UP: (1, 1), DOWN: (4, 2), DIR_DOWN: (5, 3)}[kind]
                if way == "Z":
                    src, dst = p.at[n, pl.ds(first, 2), size], zin.at[it, n, pl.ds(at, 2), size]
                else:
                    src, dst = p.at[n, first, size], zin.at[it, n, at, size]
            to = above if kind in (UP, DIR_UP, COMB_UP) else below
            return remote(src, dst, z_send.at[it], z_recv.at[it, q, kind], team=to)

        def far(q):
            z_copy(UP, q).start()
            z_copy(DOWN, q).start()

        def near(q):
            z_copy(DIR_UP, q).start()
            z_copy(DIR_DOWN, q).start()

        def combine(q):
            for w in range(2):
                z_copy((UP, DOWN)[w], q).wait_recv()
                if chunks[q][2] == "Y":
                    part = half(w, q)
                    mine = ysum[it, n_of(q), (1, 3)[w], part]
                else:
                    part = rows(q)
                    mine = p[n_of(q), TERM[w, (1, 3)[w]], part]
                total = mine.astype(F32) + zin[it, n_of(q), 2 * w, part].astype(F32)
                zout[it, n_of(q), w, part] = total.astype(BF16)
                z_copy((COMB_UP, COMB_DOWN)[w], q).start()

        def z_arrived(q):
            for w in range(2):
                if chunks[q][2] != "Z":
                    z_copy((DIR_UP, DIR_DOWN)[w], q).wait_recv()
                z_copy((COMB_UP, COMB_DOWN)[w], q).wait_recv()

        def z_sum(w, q):
            if chunks[q][2] == "Y":
                part = half(w, q)
                mine = ysum[it, n_of(q), 0, part]
            else:
                part = rows(q)
                mine = p[n_of(q), TERM[w, 0], part]
            arrived = [zin[it, n_of(q), k, part].astype(F32) for k in ((3, 1)[w], 4 + w)]
            return mine.astype(F32) + arrived[0] + arrived[1]

        def y_copy(q):
            if chunks[q][2] == "Y":
                src, dst = p.at[n_of(q), pl.ds(1, 4), rows(q)], yall.at[it, n_of(q), :, rows(q)]
            else:
                src, dst = yout.at[it, n_of(q), rows(q)], yin.at[it, n_of(q), rows(q)]
            return remote(src, dst, z_send.at[it], y_recv.at[it, q], team=beside)

        def across(q):
            z_arrived(q)
            yout[it, n_of(q), rows(q)] = z_sum(1, q).astype(BF16)
            y_copy(q).start()

        def across_first(q):
            y_copy(q).start()

        def around(q):
            y_copy(q).wait_recv()
            for k, dz in enumerate((1, 3, 0, 2)):
                total = p[n_of(q), TERM[0, dz], rows(q)].astype(F32) + yall[it, n_of(q), k, rows(q)].astype(F32)
                ysum[it, n_of(q), dz, rows(q)] = total.astype(BF16)
            far(q)
            near(q)

        def spot(q):
            first, size = chunks[q][:2]
            return first // BLK, pl.ds(first % BLK, size)

        def g_copy(kind, q, of, to):
            h, at = spot(q)
            (sx, sy), (dx, dy) = of, PLACE[kind]
            return remote(
                nxt[n_of(q)].at[sx, sy, h, at], nxt[n_of(q)].at[dx, dy, h, at], g_send.at[it], g_recv.at[it, q, kind], rep=to
            )

        def s_copy(k, q):
            h, at = spot(q)
            first, count = (((0, 1), (1, 3)) if chunks[q][3] == 2 else ((0, 1), (3, 1), (1, 1), (2, 1)))[k]
            return remote(
                nxt[n_of(q)].at[pl.ds(first, count), :, h, at], nxt[n_of(q)].at[pl.ds(4 + first, count), :, h, at],
                g_send.at[it], s_recv.at[it, q, k], rep=twin,
            )

        def finish(q):
            if chunks[q][2] == "Y":
                z_arrived(q)
                sums = jnp.concatenate([z_sum(0, q), z_sum(1, q)], axis=0)
            else:
                y_copy(q).wait_recv()
                sums = z_sum(0, q) + yin[it, n_of(q), rows(q)].astype(F32)
            h, at = spot(q)
            seeded = xs[0][n_of(q)][0, 0, h, at].astype(F32)
            blended = 0.9 * sums + 0.1 * seeded
            left_half, right_half = blended[:, : HALF // 2], blended[:, HALF // 2 :]
            squares[n_of(q), rows(q)] = left_half * left_half + right_half * right_half
            if nxt is None:
                kept[n_of(q), rows(q)] = blended
                return
            nxt[n_of(q)][0, 0, h, at] = blended.astype(BF16)
            g_copy(PARTNER, q, (0, 0), partner).start()
            g_copy(LEFT, q, (0, 0), right).start()
            g_copy(RIGHT, q, (0, 0), left).start()

        def got(kind, q):
            g_copy(kind, q, (0, 0), partner).wait_recv()

        def spread_partner(q):
            got(PARTNER, q)
            g_copy(LEFT_P, q, (0, 1), right).start()
            g_copy(RIGHT_P, q, (0, 1), left).start()
            s_copy(0, q).start()

        def spread_left(q):
            got(LEFT, q)
            g_copy(FAR, q, (3, 0), right).start()

        def spread_right(q):
            got(RIGHT_P, q)
            g_copy(FAR_P, q, (1, 1), left).start()

        def share_left(q):
            got(LEFT_P, q)
            s_copy(1, q).start()

        def share_right(q):
            got(RIGHT, q)
            s_copy(2, q).start()

        def share_far(q):
            kinds = (LEFT_P, RIGHT, FAR, FAR_P) if chunks[q][3] == 2 else (FAR, FAR_P)
            for kind in kinds:
                got(kind, q)
            s_copy(chunks[q][3] - 1, q).start()

        def v_copy(k):
            dc, dx, dyh = others[k]
            at = dc * 8 + (4 - dx) % 4 * 2 + dyh
            own = scales[it].at[0]
            return remote(own, scales[it].at[at], v_send.at[it], v_recv.at[it, k], rep=rep_of(dx, dyh, dc))

        def send_scales(_):
            diagonal = lax.broadcasted_iota(jnp.int32, (BLK, BLK), 0) == lax.broadcasted_iota(jnp.int32, (BLK, BLK), 1)
            for h in range(2):
                at = pl.ds(h * BLK, BLK)
                mean = jnp.sum(squares[0, at] + squares[1, at], axis=-1, keepdims=True) / C
                scale = lax.rsqrt(mean + 1e-6)
                if nxt is None:
                    for n in range(2):
                        out[at, n * HALF : (n + 1) * HALF] = (kept[n, at] * scale).astype(BF16)
                else:
                    scales[it][0, pl.ds(h, 1)] = jnp.sum(jnp.where(diagonal, scale, 0.0), axis=0, keepdims=True)
            if nxt is not None:
                for k in range(N_REP - 1):
                    v_copy(k).start()

        def take_scales(_):
            for k in range(N_REP - 1):
                v_copy(k).wait_recv()

        def take_shares(n):
            for q in range(NQ):
                if n_of(q) == n:
                    for k in range(chunks[q][3]):
                        s_copy(k, q).wait_recv()

        return dict(
            m=functools.partial(products, (2,)), n=functools.partial(products, (1, 3)), o=functools.partial(products, (0,)),
            F=far, N=near, C=combine, A=across, Y=across_first, W=around, E=finish,
            P=spread_partner, L=spread_left, M=spread_right, K=share_left, R=share_right, S=share_far,
            V=send_scales, U=take_scales, X=take_shares,
        )

    steps = [steps_of(it) for it in range(ITERS)]
    for step, it, q in ORDER:
        steps[it][step](q)

    remote(lab_all.at[pl.ds(1, N_REP - 1)], lab_all.at[pl.ds(1, N_REP - 1)], lab_send, lab_recv.at[0], rep=twin).wait_send()
    for it in range(ITERS):
        sent = ps[it].at[:, pl.ds(0, 7)]
        remote(sent, sent, z_send.at[it], y_recv.at[it, 0], team=beside).wait_send()
        if it + 1 < ITERS:
            sent = zin.at[:, :, pl.ds(0, 5)]
            remote(sent, sent, g_send.at[it], g_recv.at[it, 0, 0], rep=twin).wait_send()
            sent = scales[it].at[pl.ds(1, N_REP - 1)]
            remote(sent, sent, v_send.at[it], v_recv.at[it, 0], rep=twin).wait_send()


def on_device(affinity, col_index, labels):
    vmem = pl.BlockSpec(memory_space=pltpu.VMEM)
    dma = pltpu.SemaphoreType.DMA
    scores = pltpu.VMEM((8, 2, 2, BLK, HALF), BF16)
    partials = pltpu.VMEM((2, 8, ROWS, HALF), BF16)
    return pl.pallas_call(
        kernel,
        out_shape=jax.ShapeDtypeStruct((ROWS, C), BF16),
        in_specs=[pl.BlockSpec(memory_space=pl.ANY), pl.BlockSpec(memory_space=pltpu.SMEM), vmem],
        out_specs=vmem,
        scratch_shapes=[
            pltpu.VMEM((16, KB, BLK, BLK), BF16),
            pltpu.VMEM((8, 2, KB, BLK, BLK), BF16),
            pltpu.VMEM((N_REP, 2, BLK), jnp.int32),
            scores, scores, scores, scores, scores, scores,
            partials, partials, partials,
            pltpu.VMEM((ITERS, 2, 6, ROWS, HALF), BF16),
            pltpu.VMEM((ITERS, 2, ROWS, HALF), BF16),
            pltpu.VMEM((ITERS, 2, 2, ROWS, HALF), BF16),
            pltpu.VMEM((ITERS, 2, ROWS, HALF), BF16),
            pltpu.VMEM((ITERS, 2, 4, ROWS, HALF), BF16),
            pltpu.VMEM((ITERS, 2, 4, ROWS, HALF), BF16),
            pltpu.VMEM((2, ROWS, HALF // 2), F32),
            pltpu.VMEM((2, ROWS, HALF), F32),
            pltpu.VMEM((N_REP, 2, BLK), F32), pltpu.VMEM((N_REP, 2, BLK), F32),
            dma,
            dma, dma((N_REP - 1,)),
            dma((ITERS,)), dma((ITERS, NQ, 6)),
            dma((ITERS, NQ)),
            dma((ITERS - 1,)), dma((ITERS - 1, NQ, 7)),
            dma((ITERS - 1, NQ, 4)),
            dma((ITERS - 1,)), dma((ITERS - 1, N_REP - 1)),
        ],
        compiler_params=pltpu.CompilerParams(
            collective_id=0, has_side_effects=True, vmem_limit_bytes=50 * 2**20
        ),
    )(affinity[0], col_index[0].T, labels.reshape(2, BLK))


def solution(mesh):
    in_specs = (P("team", "rep", None, None, None), P("team", "rep", None), P(("rep", "team")))
    out_specs = P(("rep", "team"), None)
    return jax.shard_map(
        on_device, mesh=mesh, in_specs=in_specs, out_specs=out_specs, check_vma=False
    )
```

```python
import functools

import jax
import jax.numpy as jnp
from jax import lax
from jax.experimental import pallas as pl
from jax.experimental.pallas import tpu as pltpu
from jax.sharding import PartitionSpec as P

C = 512
BLK = 128
KB = 8
ITERS = 3
ROWS = 256
N_REP = 16
MESH = pl.DeviceIdType.MESH
F32 = jnp.float32
BF16 = jnp.bfloat16

CHUNKS = (
    ((0, 128, "S", 2, 0), (128, 128, "S", 2, 0), (0, 128, "S", 2, 1), (128, 128, "S", 2, 1),),
    ((0, 128, "S", 2, 0), (128, 128, "S", 2, 0), (0, 128, "S", 2, 1), (128, 128, "S", 2, 1),),
    ((0, 128, "S", 2, 0), (128, 128, "S", 2, 0), (0, 128, "Y", 2, 1), (128, 128, "S", 2, 1),),
)
ORDER = (
    ("m", 0, 0), ("F", 0, 0), ("n", 0, 0), ("N", 0, 0), ("F", 0, 1), ("C", 0, 0), ("m", 0, 1), ("o", 0, 0),
    ("N", 0, 1), ("C", 0, 1), ("A", 0, 0), ("F", 0, 2), ("n", 0, 1), ("N", 0, 2), ("A", 0, 1), ("F", 0, 3),
    ("E", 0, 0), ("C", 0, 2), ("o", 0, 1), ("N", 0, 3), ("E", 0, 1), ("C", 0, 3), ("P", 0, 0), ("A", 0, 2),
    ("L", 0, 0), ("P", 0, 1), ("L", 0, 1), ("A", 0, 3), ("M", 0, 0), ("M", 0, 1), ("E", 0, 2), ("E", 0, 3),
    ("V", 0, 0), ("S", 0, 0), ("S", 0, 1), ("P", 0, 2), ("P", 0, 3), ("L", 0, 2), ("L", 0, 3), ("X", 0, 0),
    ("U", 0, 0), ("m", 1, 0), ("M", 0, 2), ("F", 1, 0), ("M", 0, 3), ("F", 1, 1), ("n", 1, 0), ("N", 1, 0),
    ("S", 0, 2), ("C", 1, 0), ("S", 0, 3), ("C", 1, 1), ("N", 1, 1), ("o", 1, 0), ("X", 0, 1), ("m", 1, 1),
    ("A", 1, 0), ("F", 1, 2), ("n", 1, 1), ("N", 1, 2), ("A", 1, 1), ("F", 1, 3), ("E", 1, 0), ("C", 1, 2),
    ("o", 1, 1), ("N", 1, 3), ("E", 1, 1), ("C", 1, 3), ("P", 1, 0), ("A", 1, 2), ("L", 1, 0), ("P", 1, 1),
    ("A", 1, 3), ("M", 1, 0), ("L", 1, 1), ("E", 1, 2), ("M", 1, 1), ("E", 1, 3), ("V", 1, 0), ("P", 1, 2),
    ("S", 1, 0), ("L", 1, 2), ("P", 1, 3), ("S", 1, 1), ("M", 1, 2), ("U", 1, 0), ("X", 1, 0), ("L", 1, 3),
    ("M", 1, 3), ("m", 2, 0), ("n", 2, 0), ("S", 1, 2), ("F", 2, 1), ("N", 2, 1), ("S", 1, 3), ("o", 2, 0),
    ("F", 2, 0), ("N", 2, 0), ("X", 1, 1), ("m", 2, 1), ("n", 2, 1), ("o", 2, 1), ("Y", 2, 2), ("F", 2, 3),
    ("C", 2, 1), ("C", 2, 0), ("C", 2, 3), ("N", 2, 3), ("A", 2, 1), ("A", 2, 0), ("W", 2, 2), ("A", 2, 3),
    ("E", 2, 1), ("C", 2, 2), ("E", 2, 0), ("E", 2, 3), ("E", 2, 2), ("V", 2, 0),
)
NQ = len(CHUNKS[0])
HALF = C // 2

TERM = {(0, 2): 0, (1, 1): 1, (1, 3): 2, (1, 0): 3, (1, 2): 4, (0, 3): 5, (0, 1): 6, (0, 0): 7}
UP, DOWN, DIR_UP, DIR_DOWN, COMB_UP, COMB_DOWN = range(6)
PARTNER, LEFT, RIGHT, LEFT_P, RIGHT_P, FAR, FAR_P = range(7)
PLACE = {PARTNER: (0, 1), LEFT: (3, 0), RIGHT: (1, 0), LEFT_P: (3, 1), RIGHT_P: (1, 1), FAR: (2, 0), FAR_P: (2, 1)}


def kernel(
    aff_hbm, col, lab, out,
    aff, scaled, lab_all, x0a, x0b, x1a, x1b, x2a, x2b, p0, p1, p2, zin, yin, zout, yout, yall, ysum, squares, kept,
    scale0, scale1,
    aff_sem, lab_send, lab_recv, z_send, z_recv, y_recv, g_send, g_recv, s_recv, v_send, v_recv,
):
    r, t = lax.axis_index("rep"), lax.axis_index("team")
    x, yh, c = r // 4, (r // 2) % 2, r % 2
    yl, z = t // 4, t % 4

    def rep_of(dx=0, dyh=0, dc=0):
        return lax.rem(x + dx, 4) * 4 + lax.rem(yh + dyh, 2) * 2 + lax.rem(c + dc, 2)

    def team_of(dyl=0, dz=0):
        return lax.rem(yl + dyl, 2) * 4 + lax.rem(z + dz, 4)

    above, below, beside = team_of(dz=1), team_of(dz=3), team_of(dyl=1)
    right, left, partner, twin = rep_of(dx=1), rep_of(dx=3), rep_of(dyh=1), rep_of(dc=1)

    def remote(src, dst, send, recv, rep=None, team=None):
        return pltpu.make_async_remote_copy(
            src_ref=src, dst_ref=dst, send_sem=send, recv_sem=recv,
            device_id={"team": t if team is None else team, "rep": r if rep is None else rep},
            device_id_type=MESH,
        )

    xs, ps, scales = ((x0a, x0b), (x1a, x1b), (x2a, x2b)), (p0, p1, p2), (scale0, scale1)

    fetch = pltpu.make_async_copy(aff_hbm, aff, aff_sem)
    fetch.start()

    barrier = pltpu.get_barrier_semaphore()
    others = [(dc, dx, dyh) for dc in range(2) for dx in range(4) for dyh in range(2)][1:]
    others.sort(key=lambda o: -min(o[1], 4 - o[1]) - 2 * o[2])
    for dc, dx, dyh in others:
        pl.semaphore_signal(
            barrier, inc=1, device_id={"team": t, "rep": rep_of(dx, dyh, dc)}, device_id_type=MESH
        )
    for other in (above, below, beside):
        pl.semaphore_signal(barrier, inc=1, device_id={"team": other, "rep": r}, device_id_type=MESH)
    pl.semaphore_wait(barrier, N_REP - 1 + 3)

    lab_copies = []
    for k, (dc, dx, dyh) in enumerate(others):
        at = dc * 8 + (4 - dx) % 4 * 2 + dyh
        lab_copies.append(
            remote(lab, lab_all.at[at], lab_send, lab_recv.at[k], rep=rep_of(dx, dyh, dc))
        )
        lab_copies[-1].start()
    channel = lax.broadcasted_iota(jnp.int32, (BLK, HALF), 1)

    def seed(at, rows_of):
        for h in range(2):
            label = rows_of(h)[:, None]
            for n in range(2):
                x0 = xs[0][n]
                x0[at // 2, at % 2, h] = jnp.where(label == channel + n * HALF, 16.0, 0.0).astype(BF16)

    seed(0, lambda h: lab[h])
    for k in reversed(range(N_REP - 1)):
        dc, dx, dyh = others[k]
        at = dc * 8 + (4 - dx) % 4 * 2 + dyh
        lab_copies[k].wait_recv()
        seed(at, lambda h, at=at: lab_all[at, h])
    fetch.wait()

    def steps_of(it):
        p = ps[it]
        nxt = xs[it + 1] if it + 1 < ITERS else None
        chunks = CHUNKS[it]

        def place_of(i, s):
            block = col[s, i]
            owner = lax.div(block, 2)
            dx = lax.rem(lax.div(owner, 4) + 4 - x, 4)
            dyh = lax.rem(lax.rem(lax.div(owner, 2), 2) + yh, 2)
            dc = lax.rem(lax.rem(owner, 2) + c, 2)
            return dc * 4 + dx, dyh, lax.rem(block, 2)

        def block_row(w, dz, h, n):
            i = 2 * team_of(w, dz) + h
            cur = xs[it][n]
            places = [place_of(i, s) for s in range(KB)]

            def weights(s):
                if it == 0:
                    return aff[i, s]
                if n == 1:
                    return scaled[TERM[w, dz], h, s]
                a, b, k = places[s]
                by = scales[it - 1][2 * a + b, pl.ds(k, 1)]
                product = (aff[i, s].astype(F32) * by).astype(BF16)
                scaled[TERM[w, dz], h, s] = product
                return product

            acc = None
            for s in range(0, KB, 2):
                lhs = jnp.concatenate([weights(s), weights(s + 1)], axis=1)
                rhs = jnp.concatenate([cur[places[s]], cur[places[s + 1]]], axis=0)
                d = jnp.dot(lhs, rhs, preferred_element_type=F32)
                acc = d if acc is None else acc + d
            p[n, TERM[w, dz], h * BLK : (h + 1) * BLK] = acc.astype(BF16)

        def products(dzs, n):
            for dz in dzs:
                for h in range(2):
                    for w in range(2):
                        block_row(w, dz, h, n)

        def n_of(q):
            return chunks[q][4]

        def rows(q):
            return pl.ds(chunks[q][0], chunks[q][1])

        def half(w, q):
            first, size = chunks[q][:2]
            return pl.ds(first + w * (size // 2), size // 2)

        def z_copy(kind, q):
            way, size, n = chunks[q][2], rows(q), n_of(q)
            if kind in (COMB_UP, COMB_DOWN):
                at = kind - COMB_UP
                part = half(at, q) if way == "Y" else size
                src, dst = zout.at[it, n, at, part], zin.at[it, n, kind, part]
            elif way == "Y":
                dz, part, at = {
                    UP: (2, 0, 0), DIR_UP: (1, 1, 1), DOWN: (2, 1, 2), DIR_DOWN: (3, 0, 3)
                }[kind]
                part = half(part, q)
                src, dst = ysum.at[it, n, dz, part], zin.at[it, n, at, part]
            else:
                first, at = {UP: (0, 0), DIR_UP: (1, 1), DOWN: (4, 2), DIR_DOWN: (5, 3)}[kind]
                if way == "Z":
                    src, dst = p.at[n, pl.ds(first, 2), size], zin.at[it, n, pl.ds(at, 2), size]
                else:
                    src, dst = p.at[n, first, size], zin.at[it, n, at, size]
            to = above if kind in (UP, DIR_UP, COMB_UP) else below
            return remote(src, dst, z_send.at[it], z_recv.at[it, q, kind], team=to)

        def far(q):
            z_copy(UP, q).start()
            z_copy(DOWN, q).start()

        def near(q):
            z_copy(DIR_UP, q).start()
            z_copy(DIR_DOWN, q).start()

        def combine(q):
            for w in range(2):
                z_copy((UP, DOWN)[w], q).wait_recv()
                if chunks[q][2] == "Y":
                    part = half(w, q)
                    mine = ysum[it, n_of(q), (1, 3)[w], part]
                else:
                    part = rows(q)
                    mine = p[n_of(q), TERM[w, (1, 3)[w]], part]
                total = mine.astype(F32) + zin[it, n_of(q), 2 * w, part].astype(F32)
                zout[it, n_of(q), w, part] = total.astype(BF16)
                z_copy((COMB_UP, COMB_DOWN)[w], q).start()

        def z_arrived(q):
            for w in range(2):
                if chunks[q][2] != "Z":
                    z_copy((DIR_UP, DIR_DOWN)[w], q).wait_recv()
                z_copy((COMB_UP, COMB_DOWN)[w], q).wait_recv()

        def z_sum(w, q):
            if chunks[q][2] == "Y":
                part = half(w, q)
                mine = ysum[it, n_of(q), 0, part]
            else:
                part = rows(q)
                mine = p[n_of(q), TERM[w, 0], part]
            arrived = [zin[it, n_of(q), k, part].astype(F32) for k in ((3, 1)[w], 4 + w)]
            return mine.astype(F32) + arrived[0] + arrived[1]

        def y_copy(q):
            if chunks[q][2] == "Y":
                src, dst = p.at[n_of(q), pl.ds(1, 4), rows(q)], yall.at[it, n_of(q), :, rows(q)]
            else:
                src, dst = yout.at[it, n_of(q), rows(q)], yin.at[it, n_of(q), rows(q)]
            return remote(src, dst, z_send.at[it], y_recv.at[it, q], team=beside)

        def across(q):
            z_arrived(q)
            yout[it, n_of(q), rows(q)] = z_sum(1, q).astype(BF16)
            y_copy(q).start()

        def across_first(q):
            y_copy(q).start()

        def around(q):
            y_copy(q).wait_recv()
            for k, dz in enumerate((1, 3, 0, 2)):
                total = p[n_of(q), TERM[0, dz], rows(q)].astype(F32) + yall[it, n_of(q), k, rows(q)].astype(F32)
                ysum[it, n_of(q), dz, rows(q)] = total.astype(BF16)
            far(q)
            near(q)

        def spot(q):
            first, size = chunks[q][:2]
            return first // BLK, pl.ds(first % BLK, size)

        def g_copy(kind, q, of, to):
            h, at = spot(q)
            (sx, sy), (dx, dy) = of, PLACE[kind]
            return remote(
                nxt[n_of(q)].at[sx, sy, h, at], nxt[n_of(q)].at[dx, dy, h, at], g_send.at[it], g_recv.at[it, q, kind], rep=to
            )

        def s_copy(k, q):
            h, at = spot(q)
            first, count = (((0, 1), (1, 3)) if chunks[q][3] == 2 else ((0, 1), (3, 1), (1, 1), (2, 1)))[k]
            return remote(
                nxt[n_of(q)].at[pl.ds(first, count), :, h, at], nxt[n_of(q)].at[pl.ds(4 + first, count), :, h, at],
                g_send.at[it], s_recv.at[it, q, k], rep=twin,
            )

        def finish(q):
            if chunks[q][2] == "Y":
                z_arrived(q)
                sums = jnp.concatenate([z_sum(0, q), z_sum(1, q)], axis=0)
            else:
                y_copy(q).wait_recv()
                sums = z_sum(0, q) + yin[it, n_of(q), rows(q)].astype(F32)
            h, at = spot(q)
            seeded = xs[0][n_of(q)][0, 0, h, at].astype(F32)
            blended = 0.9 * sums + 0.1 * seeded
            left_half, right_half = blended[:, : HALF // 2], blended[:, HALF // 2 :]
            squares[n_of(q), rows(q)] = left_half * left_half + right_half * right_half
            if nxt is None:
                kept[n_of(q), rows(q)] = blended
                return
            nxt[n_of(q)][0, 0, h, at] = blended.astype(BF16)
            g_copy(PARTNER, q, (0, 0), partner).start()
            g_copy(LEFT, q, (0, 0), right).start()
            g_copy(RIGHT, q, (0, 0), left).start()

        def got(kind, q):
            g_copy(kind, q, (0, 0), partner).wait_recv()

        def spread_partner(q):
            got(PARTNER, q)
            g_copy(LEFT_P, q, (0, 1), right).start()
            g_copy(RIGHT_P, q, (0, 1), left).start()
            s_copy(0, q).start()

        def spread_left(q):
            got(LEFT, q)
            g_copy(FAR, q, (3, 0), right).start()

        def spread_right(q):
            got(RIGHT_P, q)
            g_copy(FAR_P, q, (1, 1), left).start()

        def share_left(q):
            got(LEFT_P, q)
            s_copy(1, q).start()

        def share_right(q):
            got(RIGHT, q)
            s_copy(2, q).start()

        def share_far(q):
            kinds = (LEFT_P, RIGHT, FAR, FAR_P) if chunks[q][3] == 2 else (FAR, FAR_P)
            for kind in kinds:
                got(kind, q)
            s_copy(chunks[q][3] - 1, q).start()

        def v_copy(k):
            dc, dx, dyh = others[k]
            at = dc * 8 + (4 - dx) % 4 * 2 + dyh
            own = scales[it].at[0]
            return remote(own, scales[it].at[at], v_send.at[it], v_recv.at[it, k], rep=rep_of(dx, dyh, dc))

        def send_scales(_):
            diagonal = lax.broadcasted_iota(jnp.int32, (BLK, BLK), 0) == lax.broadcasted_iota(jnp.int32, (BLK, BLK), 1)
            for h in range(2):
                at = pl.ds(h * BLK, BLK)
                mean = jnp.sum(squares[0, at] + squares[1, at], axis=-1, keepdims=True) / C
                scale = lax.rsqrt(mean + 1e-6)
                if nxt is None:
                    for n in range(2):
                        out[at, n * HALF : (n + 1) * HALF] = (kept[n, at] * scale).astype(BF16)
                else:
                    scales[it][0, pl.ds(h, 1)] = jnp.sum(jnp.where(diagonal, scale, 0.0), axis=0, keepdims=True)
            if nxt is not None:
                for k in range(N_REP - 1):
                    v_copy(k).start()

        def take_scales(_):
            for k in range(N_REP - 1):
                v_copy(k).wait_recv()

        def take_shares(n):
            for q in range(NQ):
                if n_of(q) == n:
                    for k in range(chunks[q][3]):
                        s_copy(k, q).wait_recv()

        return dict(
            m=functools.partial(products, (2,)), n=functools.partial(products, (1, 3)), o=functools.partial(products, (0,)),
            F=far, N=near, C=combine, A=across, Y=across_first, W=around, E=finish,
            P=spread_partner, L=spread_left, M=spread_right, K=share_left, R=share_right, S=share_far,
            V=send_scales, U=take_scales, X=take_shares,
        )

    steps = [steps_of(it) for it in range(ITERS)]
    for step, it, q in ORDER:
        steps[it][step](q)

    remote(lab_all.at[pl.ds(1, N_REP - 1)], lab_all.at[pl.ds(1, N_REP - 1)], lab_send, lab_recv.at[0], rep=twin).wait_send()
    for it in range(ITERS):
        sent = ps[it].at[:, pl.ds(0, 7)]
        remote(sent, sent, z_send.at[it], y_recv.at[it, 0], team=beside).wait_send()
        if it + 1 < ITERS:
            sent = zin.at[:, :, pl.ds(0, 5)]
            remote(sent, sent, g_send.at[it], g_recv.at[it, 0, 0], rep=twin).wait_send()
            sent = scales[it].at[pl.ds(1, N_REP - 1)]
            remote(sent, sent, v_send.at[it], v_recv.at[it, 0], rep=twin).wait_send()


def on_device(affinity, col_index, labels):
    vmem = pl.BlockSpec(memory_space=pltpu.VMEM)
    dma = pltpu.SemaphoreType.DMA
    scores = pltpu.VMEM((8, 2, 2, BLK, HALF), BF16)
    partials = pltpu.VMEM((2, 8, ROWS, HALF), BF16)
    return pl.pallas_call(
        kernel,
        out_shape=jax.ShapeDtypeStruct((ROWS, C), BF16),
        in_specs=[pl.BlockSpec(memory_space=pl.ANY), pl.BlockSpec(memory_space=pltpu.SMEM), vmem],
        out_specs=vmem,
        scratch_shapes=[
            pltpu.VMEM((16, KB, BLK, BLK), BF16),
            pltpu.VMEM((8, 2, KB, BLK, BLK), BF16),
            pltpu.VMEM((N_REP, 2, BLK), jnp.int32),
            scores, scores, scores, scores, scores, scores,
            partials, partials, partials,
            pltpu.VMEM((ITERS, 2, 6, ROWS, HALF), BF16),
            pltpu.VMEM((ITERS, 2, ROWS, HALF), BF16),
            pltpu.VMEM((ITERS, 2, 2, ROWS, HALF), BF16),
            pltpu.VMEM((ITERS, 2, ROWS, HALF), BF16),
            pltpu.VMEM((ITERS, 2, 4, ROWS, HALF), BF16),
            pltpu.VMEM((ITERS, 2, 4, ROWS, HALF), BF16),
            pltpu.VMEM((2, ROWS, HALF // 2), F32),
            pltpu.VMEM((2, ROWS, HALF), F32),
            pltpu.VMEM((N_REP, 2, BLK), F32), pltpu.VMEM((N_REP, 2, BLK), F32),
            dma,
            dma, dma((N_REP - 1,)),
            dma((ITERS,)), dma((ITERS, NQ, 6)),
            dma((ITERS, NQ)),
            dma((ITERS - 1,)), dma((ITERS - 1, NQ, 7)),
            dma((ITERS - 1, NQ, 4)),
            dma((ITERS - 1,)), dma((ITERS - 1, N_REP - 1)),
        ],
        compiler_params=pltpu.CompilerParams(
            collective_id=0, has_side_effects=True, vmem_limit_bytes=50 * 2**20
        ),
    )(affinity[0], col_index[0].T, labels.reshape(2, BLK))


def solution(mesh):
    in_specs = (P("team", "rep", None, None, None), P("team", "rep", None), P(("rep", "team")))
    out_specs = P(("rep", "team"), None)
    return jax.shard_map(
        on_device, mesh=mesh, in_specs=in_specs, out_specs=out_specs, check_vma=False
    )
```

```python
import functools

import jax
import jax.numpy as jnp
from jax import lax
from jax.experimental import pallas as pl
from jax.experimental.pallas import tpu as pltpu
from jax.sharding import PartitionSpec as P

C = 512
BLK = 128
KB = 8
ITERS = 3
ROWS = 256
N_REP = 16
MESH = pl.DeviceIdType.MESH
F32 = jnp.float32
BF16 = jnp.bfloat16

CHUNKS = (
    ((0, 128, "S", 4, 0), (128, 128, "S", 4, 0), (0, 128, "S", 2, 1), (128, 128, "S", 2, 1),),
    ((0, 128, "S", 4, 0), (128, 128, "S", 4, 0), (0, 128, "S", 2, 1), (128, 128, "S", 2, 1),),
    ((0, 128, "S", 2, 0), (128, 128, "S", 2, 0), (0, 128, "Y", 2, 1), (128, 128, "S", 2, 1),),
)
ORDER = (
    ("m", 0, 0), ("F", 0, 0), ("n", 0, 0), ("F", 0, 1), ("m", 0, 1), ("o", 0, 0), ("N", 0, 0), ("C", 0, 0),
    ("n", 0, 1), ("C", 0, 1), ("N", 0, 1), ("A", 0, 0), ("F", 0, 2), ("o", 0, 1), ("F", 0, 3), ("A", 0, 1),
    ("N", 0, 2), ("E", 0, 0), ("N", 0, 3), ("C", 0, 2), ("E", 0, 1), ("L", 0, 0), ("C", 0, 3), ("P", 0, 0),
    ("A", 0, 2), ("P", 0, 1), ("A", 0, 3), ("L", 0, 1), ("M", 0, 0), ("K", 0, 0), ("M", 0, 1), ("E", 0, 2),
    ("E", 0, 3), ("V", 0, 0), ("S", 0, 0), ("K", 0, 1), ("R", 0, 0), ("R", 0, 1), ("S", 0, 1), ("L", 0, 2),
    ("P", 0, 2), ("L", 0, 3), ("X", 0, 0), ("P", 0, 3), ("U", 0, 0), ("m", 1, 0), ("F", 1, 0), ("M", 0, 2),
    ("M", 0, 3), ("F", 1, 1), ("n", 1, 0), ("N", 1, 0), ("C", 1, 0), ("S", 0, 2), ("S", 0, 3), ("C", 1, 1),
    ("N", 1, 1), ("o", 1, 0), ("X", 0, 1), ("m", 1, 1), ("A", 1, 0), ("F", 1, 2), ("n", 1, 1), ("N", 1, 2),
    ("A", 1, 1), ("F", 1, 3), ("E", 1, 0), ("C", 1, 2), ("o", 1, 1), ("N", 1, 3), ("E", 1, 1), ("C", 1, 3),
    ("P", 1, 0), ("L", 1, 0), ("A", 1, 2), ("L", 1, 1), ("P", 1, 1), ("A", 1, 3), ("M", 1, 0), ("E", 1, 2),
    ("K", 1, 0), ("M", 1, 1), ("E", 1, 3), ("R", 1, 0), ("V", 1, 0), ("P", 1, 2), ("K", 1, 1), ("L", 1, 2),
    ("S", 1, 0), ("R", 1, 1), ("S", 1, 1), ("P", 1, 3), ("X", 1, 0), ("M", 1, 2), ("L", 1, 3), ("U", 1, 0),
    ("M", 1, 3), ("m", 2, 0), ("n", 2, 0), ("S", 1, 2), ("F", 2, 1), ("S", 1, 3), ("F", 2, 0), ("N", 2, 0),
    ("N", 2, 1), ("o", 2, 0), ("X", 1, 1), ("m", 2, 1), ("n", 2, 1), ("o", 2, 1), ("Y", 2, 2), ("F", 2, 3),
    ("C", 2, 1), ("C", 2, 0), ("C", 2, 3), ("N", 2, 3), ("A", 2, 1), ("A", 2, 0), ("W", 2, 2), ("A", 2, 3),
    ("C", 2, 2), ("E", 2, 0), ("E", 2, 1), ("E", 2, 3), ("E", 2, 2), ("V", 2, 0),
)
NQ = len(CHUNKS[0])
HALF = C // 2

TERM = {(0, 2): 0, (1, 1): 1, (1, 3): 2, (1, 0): 3, (1, 2): 4, (0, 3): 5, (0, 1): 6, (0, 0): 7}
UP, DOWN, DIR_UP, DIR_DOWN, COMB_UP, COMB_DOWN = range(6)
PARTNER, LEFT, RIGHT, LEFT_P, RIGHT_P, FAR, FAR_P = range(7)
PLACE = {PARTNER: (0, 1), LEFT: (3, 0), RIGHT: (1, 0), LEFT_P: (3, 1), RIGHT_P: (1, 1), FAR: (2, 0), FAR_P: (2, 1)}


def kernel(
    aff_hbm, col, lab, out,
    aff, scaled, lab_all, x0a, x0b, x1a, x1b, x2a, x2b, p0, p1, p2, zin, yin, zout, yout, yall, ysum, squares, kept,
    scale0, scale1,
    aff_sem, lab_send, lab_recv, z_send, z_recv, y_recv, g_send, g_recv, s_recv, v_send, v_recv,
):
    r, t = lax.axis_index("rep"), lax.axis_index("team")
    x, yh, c = r // 4, (r // 2) % 2, r % 2
    yl, z = t // 4, t % 4

    def rep_of(dx=0, dyh=0, dc=0):
        return lax.rem(x + dx, 4) * 4 + lax.rem(yh + dyh, 2) * 2 + lax.rem(c + dc, 2)

    def team_of(dyl=0, dz=0):
        return lax.rem(yl + dyl, 2) * 4 + lax.rem(z + dz, 4)

    above, below, beside = team_of(dz=1), team_of(dz=3), team_of(dyl=1)
    right, left, partner, twin = rep_of(dx=1), rep_of(dx=3), rep_of(dyh=1), rep_of(dc=1)

    def remote(src, dst, send, recv, rep=None, team=None):
        return pltpu.make_async_remote_copy(
            src_ref=src, dst_ref=dst, send_sem=send, recv_sem=recv,
            device_id={"team": t if team is None else team, "rep": r if rep is None else rep},
            device_id_type=MESH,
        )

    xs, ps, scales = ((x0a, x0b), (x1a, x1b), (x2a, x2b)), (p0, p1, p2), (scale0, scale1)

    fetch = pltpu.make_async_copy(aff_hbm, aff, aff_sem)
    fetch.start()

    barrier = pltpu.get_barrier_semaphore()
    others = [(dc, dx, dyh) for dc in range(2) for dx in range(4) for dyh in range(2)][1:]
    others.sort(key=lambda o: -min(o[1], 4 - o[1]) - 2 * o[2])
    for dc, dx, dyh in others:
        pl.semaphore_signal(
            barrier, inc=1, device_id={"team": t, "rep": rep_of(dx, dyh, dc)}, device_id_type=MESH
        )
    for other in (above, below, beside):
        pl.semaphore_signal(barrier, inc=1, device_id={"team": other, "rep": r}, device_id_type=MESH)
    pl.semaphore_wait(barrier, N_REP - 1 + 3)

    lab_copies = []
    for k, (dc, dx, dyh) in enumerate(others):
        at = dc * 8 + (4 - dx) % 4 * 2 + dyh
        lab_copies.append(
            remote(lab, lab_all.at[at], lab_send, lab_recv.at[k], rep=rep_of(dx, dyh, dc))
        )
        lab_copies[-1].start()
    channel = lax.broadcasted_iota(jnp.int32, (BLK, HALF), 1)

    def seed(at, rows_of):
        for h in range(2):
            label = rows_of(h)[:, None]
            for n in range(2):
                x0 = xs[0][n]
                x0[at // 2, at % 2, h] = jnp.where(label == channel + n * HALF, 16.0, 0.0).astype(BF16)

    seed(0, lambda h: lab[h])
    for k in reversed(range(N_REP - 1)):
        dc, dx, dyh = others[k]
        at = dc * 8 + (4 - dx) % 4 * 2 + dyh
        lab_copies[k].wait_recv()
        seed(at, lambda h, at=at: lab_all[at, h])
    fetch.wait()

    def steps_of(it):
        p = ps[it]
        nxt = xs[it + 1] if it + 1 < ITERS else None
        chunks = CHUNKS[it]

        def place_of(i, s):
            block = col[s, i]
            owner = lax.div(block, 2)
            dx = lax.rem(lax.div(owner, 4) + 4 - x, 4)
            dyh = lax.rem(lax.rem(lax.div(owner, 2), 2) + yh, 2)
            dc = lax.rem(lax.rem(owner, 2) + c, 2)
            return dc * 4 + dx, dyh, lax.rem(block, 2)

        def block_row(w, dz, h, n):
            i = 2 * team_of(w, dz) + h
            cur = xs[it][n]
            places = [place_of(i, s) for s in range(KB)]

            def weights(s):
                if it == 0:
                    return aff[i, s]
                if n == 1:
                    return scaled[TERM[w, dz], h, s]
                a, b, k = places[s]
                by = scales[it - 1][2 * a + b, pl.ds(k, 1)]
                product = (aff[i, s].astype(F32) * by).astype(BF16)
                scaled[TERM[w, dz], h, s] = product
                return product

            acc = None
            for s in range(0, KB, 2):
                lhs = jnp.concatenate([weights(s), weights(s + 1)], axis=1)
                rhs = jnp.concatenate([cur[places[s]], cur[places[s + 1]]], axis=0)
                d = jnp.dot(lhs, rhs, preferred_element_type=F32)
                acc = d if acc is None else acc + d
            p[n, TERM[w, dz], h * BLK : (h + 1) * BLK] = acc.astype(BF16)

        def products(dzs, n):
            for dz in dzs:
                for h in range(2):
                    for w in range(2):
                        block_row(w, dz, h, n)

        def n_of(q):
            return chunks[q][4]

        def rows(q):
            return pl.ds(chunks[q][0], chunks[q][1])

        def half(w, q):
            first, size = chunks[q][:2]
            return pl.ds(first + w * (size // 2), size // 2)

        def z_copy(kind, q):
            way, size, n = chunks[q][2], rows(q), n_of(q)
            if kind in (COMB_UP, COMB_DOWN):
                at = kind - COMB_UP
                part = half(at, q) if way == "Y" else size
                src, dst = zout.at[it, n, at, part], zin.at[it, n, kind, part]
            elif way == "Y":
                dz, part, at = {
                    UP: (2, 0, 0), DIR_UP: (1, 1, 1), DOWN: (2, 1, 2), DIR_DOWN: (3, 0, 3)
                }[kind]
                part = half(part, q)
                src, dst = ysum.at[it, n, dz, part], zin.at[it, n, at, part]
            else:
                first, at = {UP: (0, 0), DIR_UP: (1, 1), DOWN: (4, 2), DIR_DOWN: (5, 3)}[kind]
                if way == "Z":
                    src, dst = p.at[n, pl.ds(first, 2), size], zin.at[it, n, pl.ds(at, 2), size]
                else:
                    src, dst = p.at[n, first, size], zin.at[it, n, at, size]
            to = above if kind in (UP, DIR_UP, COMB_UP) else below
            return remote(src, dst, z_send.at[it], z_recv.at[it, q, kind], team=to)

        def far(q):
            z_copy(UP, q).start()
            z_copy(DOWN, q).start()

        def near(q):
            z_copy(DIR_UP, q).start()
            z_copy(DIR_DOWN, q).start()

        def combine(q):
            for w in range(2):
                z_copy((UP, DOWN)[w], q).wait_recv()
                if chunks[q][2] == "Y":
                    part = half(w, q)
                    mine = ysum[it, n_of(q), (1, 3)[w], part]
                else:
                    part = rows(q)
                    mine = p[n_of(q), TERM[w, (1, 3)[w]], part]
                total = mine.astype(F32) + zin[it, n_of(q), 2 * w, part].astype(F32)
                zout[it, n_of(q), w, part] = total.astype(BF16)
                z_copy((COMB_UP, COMB_DOWN)[w], q).start()

        def z_arrived(q):
            for w in range(2):
                if chunks[q][2] != "Z":
                    z_copy((DIR_UP, DIR_DOWN)[w], q).wait_recv()
                z_copy((COMB_UP, COMB_DOWN)[w], q).wait_recv()

        def z_sum(w, q):
            if chunks[q][2] == "Y":
                part = half(w, q)
                mine = ysum[it, n_of(q), 0, part]
            else:
                part = rows(q)
                mine = p[n_of(q), TERM[w, 0], part]
            arrived = [zin[it, n_of(q), k, part].astype(F32) for k in ((3, 1)[w], 4 + w)]
            return mine.astype(F32) + arrived[0] + arrived[1]

        def y_copy(q):
            if chunks[q][2] == "Y":
                src, dst = p.at[n_of(q), pl.ds(1, 4), rows(q)], yall.at[it, n_of(q), :, rows(q)]
            else:
                src, dst = yout.at[it, n_of(q), rows(q)], yin.at[it, n_of(q), rows(q)]
            return remote(src, dst, z_send.at[it], y_recv.at[it, q], team=beside)

        def across(q):
            z_arrived(q)
            yout[it, n_of(q), rows(q)] = z_sum(1, q).astype(BF16)
            y_copy(q).start()

        def across_first(q):
            y_copy(q).start()

        def around(q):
            y_copy(q).wait_recv()
            for k, dz in enumerate((1, 3, 0, 2)):
                total = p[n_of(q), TERM[0, dz], rows(q)].astype(F32) + yall[it, n_of(q), k, rows(q)].astype(F32)
                ysum[it, n_of(q), dz, rows(q)] = total.astype(BF16)
            far(q)
            near(q)

        def spot(q):
            first, size = chunks[q][:2]
            return first // BLK, pl.ds(first % BLK, size)

        def g_copy(kind, q, of, to):
            h, at = spot(q)
            (sx, sy), (dx, dy) = of, PLACE[kind]
            return remote(
                nxt[n_of(q)].at[sx, sy, h, at], nxt[n_of(q)].at[dx, dy, h, at], g_send.at[it], g_recv.at[it, q, kind], rep=to
            )

        def s_copy(k, q):
            h, at = spot(q)
            first, count = (((0, 1), (1, 3)) if chunks[q][3] == 2 else ((0, 1), (3, 1), (1, 1), (2, 1)))[k]
            return remote(
                nxt[n_of(q)].at[pl.ds(first, count), :, h, at], nxt[n_of(q)].at[pl.ds(4 + first, count), :, h, at],
                g_send.at[it], s_recv.at[it, q, k], rep=twin,
            )

        def finish(q):
            if chunks[q][2] == "Y":
                z_arrived(q)
                sums = jnp.concatenate([z_sum(0, q), z_sum(1, q)], axis=0)
            else:
                y_copy(q).wait_recv()
                sums = z_sum(0, q) + yin[it, n_of(q), rows(q)].astype(F32)
            h, at = spot(q)
            seeded = xs[0][n_of(q)][0, 0, h, at].astype(F32)
            blended = 0.9 * sums + 0.1 * seeded
            left_half, right_half = blended[:, : HALF // 2], blended[:, HALF // 2 :]
            squares[n_of(q), rows(q)] = left_half * left_half + right_half * right_half
            if nxt is None:
                kept[n_of(q), rows(q)] = blended
                return
            nxt[n_of(q)][0, 0, h, at] = blended.astype(BF16)
            g_copy(PARTNER, q, (0, 0), partner).start()
            g_copy(LEFT, q, (0, 0), right).start()
            g_copy(RIGHT, q, (0, 0), left).start()

        def got(kind, q):
            g_copy(kind, q, (0, 0), partner).wait_recv()

        def spread_partner(q):
            got(PARTNER, q)
            g_copy(LEFT_P, q, (0, 1), right).start()
            g_copy(RIGHT_P, q, (0, 1), left).start()
            s_copy(0, q).start()

        def spread_left(q):
            got(LEFT, q)
            g_copy(FAR, q, (3, 0), right).start()

        def spread_right(q):
            got(RIGHT_P, q)
            g_copy(FAR_P, q, (1, 1), left).start()

        def share_left(q):
            got(LEFT_P, q)
            s_copy(1, q).start()

        def share_right(q):
            got(RIGHT, q)
            s_copy(2, q).start()

        def share_far(q):
            kinds = (LEFT_P, RIGHT, FAR, FAR_P) if chunks[q][3] == 2 else (FAR, FAR_P)
            for kind in kinds:
                got(kind, q)
            s_copy(chunks[q][3] - 1, q).start()

        def v_copy(k):
            dc, dx, dyh = others[k]
            at = dc * 8 + (4 - dx) % 4 * 2 + dyh
            own = scales[it].at[0]
            return remote(own, scales[it].at[at], v_send.at[it], v_recv.at[it, k], rep=rep_of(dx, dyh, dc))

        def send_scales(_):
            diagonal = lax.broadcasted_iota(jnp.int32, (BLK, BLK), 0) == lax.broadcasted_iota(jnp.int32, (BLK, BLK), 1)
            for h in range(2):
                at = pl.ds(h * BLK, BLK)
                mean = jnp.sum(squares[0, at] + squares[1, at], axis=-1, keepdims=True) / C
                scale = lax.rsqrt(mean + 1e-6)
                if nxt is None:
                    for n in range(2):
                        out[at, n * HALF : (n + 1) * HALF] = (kept[n, at] * scale).astype(BF16)
                else:
                    scales[it][0, pl.ds(h, 1)] = jnp.sum(jnp.where(diagonal, scale, 0.0), axis=0, keepdims=True)
            if nxt is not None:
                for k in range(N_REP - 1):
                    v_copy(k).start()

        def take_scales(_):
            for k in range(N_REP - 1):
                v_copy(k).wait_recv()

        def take_shares(n):
            for q in range(NQ):
                if n_of(q) == n:
                    for k in range(chunks[q][3]):
                        s_copy(k, q).wait_recv()

        return dict(
            m=functools.partial(products, (2,)), n=functools.partial(products, (1, 3)), o=functools.partial(products, (0,)),
            F=far, N=near, C=combine, A=across, Y=across_first, W=around, E=finish,
            P=spread_partner, L=spread_left, M=spread_right, K=share_left, R=share_right, S=share_far,
            V=send_scales, U=take_scales, X=take_shares,
        )

    steps = [steps_of(it) for it in range(ITERS)]
    for step, it, q in ORDER:
        steps[it][step](q)

    remote(lab_all.at[pl.ds(1, N_REP - 1)], lab_all.at[pl.ds(1, N_REP - 1)], lab_send, lab_recv.at[0], rep=twin).wait_send()
    for it in range(ITERS):
        sent = ps[it].at[:, pl.ds(0, 7)]
        remote(sent, sent, z_send.at[it], y_recv.at[it, 0], team=beside).wait_send()
        if it + 1 < ITERS:
            sent = zin.at[:, :, pl.ds(0, 5)]
            remote(sent, sent, g_send.at[it], g_recv.at[it, 0, 0], rep=twin).wait_send()
            sent = scales[it].at[pl.ds(1, N_REP - 1)]
            remote(sent, sent, v_send.at[it], v_recv.at[it, 0], rep=twin).wait_send()


def on_device(affinity, col_index, labels):
    vmem = pl.BlockSpec(memory_space=pltpu.VMEM)
    dma = pltpu.SemaphoreType.DMA
    scores = pltpu.VMEM((8, 2, 2, BLK, HALF), BF16)
    partials = pltpu.VMEM((2, 8, ROWS, HALF), BF16)
    return pl.pallas_call(
        kernel,
        out_shape=jax.ShapeDtypeStruct((ROWS, C), BF16),
        in_specs=[pl.BlockSpec(memory_space=pl.ANY), pl.BlockSpec(memory_space=pltpu.SMEM), vmem],
        out_specs=vmem,
        scratch_shapes=[
            pltpu.VMEM((16, KB, BLK, BLK), BF16),
            pltpu.VMEM((8, 2, KB, BLK, BLK), BF16),
            pltpu.VMEM((N_REP, 2, BLK), jnp.int32),
            scores, scores, scores, scores, scores, scores,
            partials, partials, partials,
            pltpu.VMEM((ITERS, 2, 6, ROWS, HALF), BF16),
            pltpu.VMEM((ITERS, 2, ROWS, HALF), BF16),
            pltpu.VMEM((ITERS, 2, 2, ROWS, HALF), BF16),
            pltpu.VMEM((ITERS, 2, ROWS, HALF), BF16),
            pltpu.VMEM((ITERS, 2, 4, ROWS, HALF), BF16),
            pltpu.VMEM((ITERS, 2, 4, ROWS, HALF), BF16),
            pltpu.VMEM((2, ROWS, HALF // 2), F32),
            pltpu.VMEM((2, ROWS, HALF), F32),
            pltpu.VMEM((N_REP, 2, BLK), F32), pltpu.VMEM((N_REP, 2, BLK), F32),
            dma,
            dma, dma((N_REP - 1,)),
            dma((ITERS,)), dma((ITERS, NQ, 6)),
            dma((ITERS, NQ)),
            dma((ITERS - 1,)), dma((ITERS - 1, NQ, 7)),
            dma((ITERS - 1, NQ, 4)),
            dma((ITERS - 1,)), dma((ITERS - 1, N_REP - 1)),
        ],
        compiler_params=pltpu.CompilerParams(
            collective_id=0, has_side_effects=True, vmem_limit_bytes=50 * 2**20
        ),
    )(affinity[0], col_index[0].T, labels.reshape(2, BLK))


def solution(mesh):
    in_specs = (P("team", "rep", None, None, None), P("team", "rep", None), P(("rep", "team")))
    out_specs = P(("rep", "team"), None)
    return jax.shard_map(
        on_device, mesh=mesh, in_specs=in_specs, out_specs=out_specs, check_vma=False
    )
```

```python
import functools

import jax
import jax.numpy as jnp
from jax import lax
from jax.experimental import pallas as pl
from jax.experimental.pallas import tpu as pltpu
from jax.sharding import PartitionSpec as P

C = 512
BLK = 128
KB = 8
ITERS = 3
ROWS = 256
N_REP = 16
MESH = pl.DeviceIdType.MESH
F32 = jnp.float32
BF16 = jnp.bfloat16

CHUNKS = (
    ((0, 128, "S", 4, 0), (128, 128, "S", 4, 0), (0, 128, "S", 2, 1), (128, 128, "S", 2, 1),),
    ((0, 128, "S", 4, 0), (128, 128, "S", 4, 0), (0, 128, "S", 2, 1), (128, 128, "S", 2, 1),),
    ((0, 128, "S", 2, 0), (128, 128, "Z", 2, 0), (0, 128, "Y", 2, 1), (128, 128, "Z", 2, 1),),
)
ORDER = (
    ("m", 0, 0), ("F", 0, 0), ("n", 0, 0), ("N", 0, 0), ("F", 0, 1), ("m", 0, 1), ("C", 0, 0), ("N", 0, 1),
    ("o", 0, 0), ("C", 0, 1), ("n", 0, 1), ("F", 0, 2), ("A", 0, 0), ("F", 0, 3), ("N", 0, 2), ("A", 0, 1),
    ("N", 0, 3), ("E", 0, 0), ("C", 0, 2), ("E", 0, 1), ("o", 0, 1), ("C", 0, 3), ("P", 0, 0), ("A", 0, 2),
    ("P", 0, 1), ("A", 0, 3), ("L", 0, 0), ("M", 0, 0), ("L", 0, 1), ("K", 0, 0), ("M", 0, 1), ("E", 0, 2),
    ("R", 0, 1), ("E", 0, 3), ("V", 0, 0), ("K", 0, 1), ("S", 0, 0), ("R", 0, 0), ("S", 0, 1), ("P", 0, 2),
    ("X", 0, 0), ("P", 0, 3), ("L", 0, 2), ("L", 0, 3), ("U", 0, 0), ("m", 1, 0), ("F", 1, 0), ("M", 0, 2),
    ("M", 0, 3), ("F", 1, 1), ("n", 1, 0), ("N", 1, 0), ("C", 1, 0), ("S", 0, 2), ("S", 0, 3), ("C", 1, 1),
    ("o", 1, 0), ("N", 1, 1), ("X", 0, 1), ("m", 1, 1), ("A", 1, 0), ("F", 1, 2), ("n", 1, 1), ("N", 1, 2),
    ("A", 1, 1), ("F", 1, 3), ("E", 1, 0), ("C", 1, 2), ("o", 1, 1), ("N", 1, 3), ("E", 1, 1), ("C", 1, 3),
    ("P", 1, 0), ("L", 1, 0), ("A", 1, 2), ("P", 1, 1), ("A", 1, 3), ("M", 1, 0), ("L", 1, 1), ("K", 1, 0),
    ("E", 1, 2), ("R", 1, 0), ("M", 1, 1), ("E", 1, 3), ("R", 1, 1), ("V", 1, 0), ("P", 1, 2), ("K", 1, 1),
    ("S", 1, 0), ("L", 1, 2), ("S", 1, 1), ("P", 1, 3), ("L", 1, 3), ("X", 1, 0), ("M", 1, 2), ("U", 1, 0),
    ("m", 2, 0), ("M", 1, 3), ("F", 2, 0), ("n", 2, 0), ("N", 2, 0), ("S", 1, 2), ("S", 1, 3), ("F", 2, 1),
    ("C", 2, 0), ("o", 2, 0), ("X", 1, 1), ("m", 2, 1), ("n", 2, 1), ("o", 2, 1), ("Y", 2, 2), ("F", 2, 3),
    ("C", 2, 1), ("C", 2, 3), ("A", 2, 1), ("A", 2, 0), ("W", 2, 2), ("A", 2, 3), ("C", 2, 2), ("E", 2, 0),
    ("E", 2, 3), ("E", 2, 1), ("E", 2, 2), ("V", 2, 0),
)
NQ = len(CHUNKS[0])
HALF = C // 2

TERM = {(0, 2): 0, (1, 1): 1, (1, 3): 2, (1, 0): 3, (1, 2): 4, (0, 3): 5, (0, 1): 6, (0, 0): 7}
UP, DOWN, DIR_UP, DIR_DOWN, COMB_UP, COMB_DOWN = range(6)
PARTNER, LEFT, RIGHT, LEFT_P, RIGHT_P, FAR, FAR_P = range(7)
PLACE = {PARTNER: (0, 1), LEFT: (3, 0), RIGHT: (1, 0), LEFT_P: (3, 1), RIGHT_P: (1, 1), FAR: (2, 0), FAR_P: (2, 1)}


def kernel(
    aff_hbm, col, lab, out,
    aff, scaled, lab_all, x0a, x0b, x1a, x1b, x2a, x2b, p0, p1, p2, zin, yin, zout, yout, yall, ysum, squares, kept,
    scale0, scale1,
    aff_sem, lab_send, lab_recv, z_send, z_recv, y_recv, g_send, g_recv, s_recv, v_send, v_recv,
):
    r, t = lax.axis_index("rep"), lax.axis_index("team")
    x, yh, c = r // 4, (r // 2) % 2, r % 2
    yl, z = t // 4, t % 4

    def rep_of(dx=0, dyh=0, dc=0):
        return lax.rem(x + dx, 4) * 4 + lax.rem(yh + dyh, 2) * 2 + lax.rem(c + dc, 2)

    def team_of(dyl=0, dz=0):
        return lax.rem(yl + dyl, 2) * 4 + lax.rem(z + dz, 4)

    above, below, beside = team_of(dz=1), team_of(dz=3), team_of(dyl=1)
    right, left, partner, twin = rep_of(dx=1), rep_of(dx=3), rep_of(dyh=1), rep_of(dc=1)

    def remote(src, dst, send, recv, rep=None, team=None):
        return pltpu.make_async_remote_copy(
            src_ref=src, dst_ref=dst, send_sem=send, recv_sem=recv,
            device_id={"team": t if team is None else team, "rep": r if rep is None else rep},
            device_id_type=MESH,
        )

    xs, ps, scales = ((x0a, x0b), (x1a, x1b), (x2a, x2b)), (p0, p1, p2), (scale0, scale1)

    fetch = pltpu.make_async_copy(aff_hbm, aff, aff_sem)
    fetch.start()

    barrier = pltpu.get_barrier_semaphore()
    others = [(dc, dx, dyh) for dc in range(2) for dx in range(4) for dyh in range(2)][1:]
    others.sort(key=lambda o: -min(o[1], 4 - o[1]) - 2 * o[2])
    for dc, dx, dyh in others:
        pl.semaphore_signal(
            barrier, inc=1, device_id={"team": t, "rep": rep_of(dx, dyh, dc)}, device_id_type=MESH
        )
    for other in (above, below, beside):
        pl.semaphore_signal(barrier, inc=1, device_id={"team": other, "rep": r}, device_id_type=MESH)
    channel = lax.broadcasted_iota(jnp.int32, (BLK, HALF), 1)

    def seed(at, rows_of):
        for h in range(2):
            label = rows_of(h)[:, None]
            for n in range(2):
                x0 = xs[0][n]
                x0[at // 2, at % 2, h] = jnp.where(label == channel + n * HALF, 16.0, 0.0).astype(BF16)

    seed(0, lambda h: lab[h])
    pl.semaphore_wait(barrier, N_REP - 1 + 3)

    lab_copies = []
    for k, (dc, dx, dyh) in enumerate(others):
        at = dc * 8 + (4 - dx) % 4 * 2 + dyh
        lab_copies.append(
            remote(lab, lab_all.at[at], lab_send, lab_recv.at[k], rep=rep_of(dx, dyh, dc))
        )
        lab_copies[-1].start()
    for k in reversed(range(N_REP - 1)):
        dc, dx, dyh = others[k]
        at = dc * 8 + (4 - dx) % 4 * 2 + dyh
        lab_copies[k].wait_recv()
        seed(at, lambda h, at=at: lab_all[at, h])
    fetch.wait()

    def steps_of(it):
        p = ps[it]
        nxt = xs[it + 1] if it + 1 < ITERS else None
        chunks = CHUNKS[it]

        def place_of(i, s):
            block = col[s, i]
            owner = lax.div(block, 2)
            dx = lax.rem(lax.div(owner, 4) + 4 - x, 4)
            dyh = lax.rem(lax.rem(lax.div(owner, 2), 2) + yh, 2)
            dc = lax.rem(lax.rem(owner, 2) + c, 2)
            return dc * 4 + dx, dyh, lax.rem(block, 2)

        def block_row(w, dz, h, n):
            i = 2 * team_of(w, dz) + h
            cur = xs[it][n]
            places = [place_of(i, s) for s in range(KB)]

            def weights(s):
                if it == 0:
                    return aff[i, s]
                if n == 1:
                    return scaled[TERM[w, dz], h, s]
                a, b, k = places[s]
                by = scales[it - 1][2 * a + b, pl.ds(k, 1)]
                product = (aff[i, s].astype(F32) * by).astype(BF16)
                scaled[TERM[w, dz], h, s] = product
                return product

            acc = None
            for s in range(0, KB, 2):
                lhs = jnp.concatenate([weights(s), weights(s + 1)], axis=1)
                rhs = jnp.concatenate([cur[places[s]], cur[places[s + 1]]], axis=0)
                d = jnp.dot(lhs, rhs, preferred_element_type=F32)
                acc = d if acc is None else acc + d
            p[n, TERM[w, dz], h * BLK : (h + 1) * BLK] = acc.astype(BF16)

        def products(dzs, n):
            for dz in dzs:
                for h in range(2):
                    for w in range(2):
                        block_row(w, dz, h, n)

        def n_of(q):
            return chunks[q][4]

        def rows(q):
            return pl.ds(chunks[q][0], chunks[q][1])

        def half(w, q):
            first, size = chunks[q][:2]
            return pl.ds(first + w * (size // 2), size // 2)

        def z_copy(kind, q):
            way, size, n = chunks[q][2], rows(q), n_of(q)
            if kind in (COMB_UP, COMB_DOWN):
                at = kind - COMB_UP
                part = half(at, q) if way == "Y" else size
                src, dst = zout.at[it, n, at, part], zin.at[it, n, kind, part]
            elif way == "Y":
                dz, part, at = {
                    UP: (2, 0, 0), DIR_UP: (1, 1, 1), DOWN: (2, 1, 2), DIR_DOWN: (3, 0, 3)
                }[kind]
                part = half(part, q)
                src, dst = ysum.at[it, n, dz, part], zin.at[it, n, at, part]
            else:
                first, at = {UP: (0, 0), DIR_UP: (1, 1), DOWN: (4, 2), DIR_DOWN: (5, 3)}[kind]
                if way == "Z":
                    src, dst = p.at[n, pl.ds(first, 2), size], zin.at[it, n, pl.ds(at, 2), size]
                else:
                    src, dst = p.at[n, first, size], zin.at[it, n, at, size]
            to = above if kind in (UP, DIR_UP, COMB_UP) else below
            return remote(src, dst, z_send.at[it], z_recv.at[it, q, kind], team=to)

        def far(q):
            z_copy(UP, q).start()
            z_copy(DOWN, q).start()

        def near(q):
            z_copy(DIR_UP, q).start()
            z_copy(DIR_DOWN, q).start()

        def combine(q):
            for w in range(2):
                z_copy((UP, DOWN)[w], q).wait_recv()
                if chunks[q][2] == "Y":
                    part = half(w, q)
                    mine = ysum[it, n_of(q), (1, 3)[w], part]
                else:
                    part = rows(q)
                    mine = p[n_of(q), TERM[w, (1, 3)[w]], part]
                total = mine.astype(F32) + zin[it, n_of(q), 2 * w, part].astype(F32)
                zout[it, n_of(q), w, part] = total.astype(BF16)
                z_copy((COMB_UP, COMB_DOWN)[w], q).start()

        def z_arrived(q):
            for w in range(2):
                if chunks[q][2] != "Z":
                    z_copy((DIR_UP, DIR_DOWN)[w], q).wait_recv()
                z_copy((COMB_UP, COMB_DOWN)[w], q).wait_recv()

        def z_sum(w, q):
            if chunks[q][2] == "Y":
                part = half(w, q)
                mine = ysum[it, n_of(q), 0, part]
            else:
                part = rows(q)
                mine = p[n_of(q), TERM[w, 0], part]
            arrived = [zin[it, n_of(q), k, part].astype(F32) for k in ((3, 1)[w], 4 + w)]
            return mine.astype(F32) + arrived[0] + arrived[1]

        def y_copy(q):
            if chunks[q][2] == "Y":
                src, dst = p.at[n_of(q), pl.ds(1, 4), rows(q)], yall.at[it, n_of(q), :, rows(q)]
            else:
                src, dst = yout.at[it, n_of(q), rows(q)], yin.at[it, n_of(q), rows(q)]
            return remote(src, dst, z_send.at[it], y_recv.at[it, q], team=beside)

        def across(q):
            z_arrived(q)
            yout[it, n_of(q), rows(q)] = z_sum(1, q).astype(BF16)
            y_copy(q).start()

        def across_first(q):
            y_copy(q).start()

        def around(q):
            y_copy(q).wait_recv()
            for k, dz in enumerate((1, 3, 0, 2)):
                total = p[n_of(q), TERM[0, dz], rows(q)].astype(F32) + yall[it, n_of(q), k, rows(q)].astype(F32)
                ysum[it, n_of(q), dz, rows(q)] = total.astype(BF16)
            far(q)
            near(q)

        def spot(q):
            first, size = chunks[q][:2]
            return first // BLK, pl.ds(first % BLK, size)

        def g_copy(kind, q, of, to):
            h, at = spot(q)
            (sx, sy), (dx, dy) = of, PLACE[kind]
            return remote(
                nxt[n_of(q)].at[sx, sy, h, at], nxt[n_of(q)].at[dx, dy, h, at], g_send.at[it], g_recv.at[it, q, kind], rep=to
            )

        def s_copy(k, q):
            h, at = spot(q)
            first, count = (((0, 1), (1, 3)) if chunks[q][3] == 2 else ((0, 1), (3, 1), (1, 1), (2, 1)))[k]
            return remote(
                nxt[n_of(q)].at[pl.ds(first, count), :, h, at], nxt[n_of(q)].at[pl.ds(4 + first, count), :, h, at],
                g_send.at[it], s_recv.at[it, q, k], rep=twin,
            )

        def finish(q):
            if chunks[q][2] == "Y":
                z_arrived(q)
                sums = jnp.concatenate([z_sum(0, q), z_sum(1, q)], axis=0)
            else:
                y_copy(q).wait_recv()
                sums = z_sum(0, q) + yin[it, n_of(q), rows(q)].astype(F32)
            h, at = spot(q)
            seeded = xs[0][n_of(q)][0, 0, h, at].astype(F32)
            blended = 0.9 * sums + 0.1 * seeded
            left_half, right_half = blended[:, : HALF // 2], blended[:, HALF // 2 :]
            squares[n_of(q), rows(q)] = left_half * left_half + right_half * right_half
            if nxt is None:
                kept[n_of(q), rows(q)] = blended
                return
            nxt[n_of(q)][0, 0, h, at] = blended.astype(BF16)
            g_copy(PARTNER, q, (0, 0), partner).start()
            g_copy(LEFT, q, (0, 0), right).start()
            g_copy(RIGHT, q, (0, 0), left).start()

        def got(kind, q):
            g_copy(kind, q, (0, 0), partner).wait_recv()

        def spread_partner(q):
            got(PARTNER, q)
            g_copy(LEFT_P, q, (0, 1), right).start()
            g_copy(RIGHT_P, q, (0, 1), left).start()
            s_copy(0, q).start()

        def spread_left(q):
            got(LEFT, q)
            g_copy(FAR, q, (3, 0), right).start()

        def spread_right(q):
            got(RIGHT_P, q)
            g_copy(FAR_P, q, (1, 1), left).start()

        def share_left(q):
            got(LEFT_P, q)
            s_copy(1, q).start()

        def share_right(q):
            got(RIGHT, q)
            s_copy(2, q).start()

        def share_far(q):
            kinds = (LEFT_P, RIGHT, FAR, FAR_P) if chunks[q][3] == 2 else (FAR, FAR_P)
            for kind in kinds:
                got(kind, q)
            s_copy(chunks[q][3] - 1, q).start()

        def v_copy(k):
            dc, dx, dyh = others[k]
            at = dc * 8 + (4 - dx) % 4 * 2 + dyh
            own = scales[it].at[0]
            return remote(own, scales[it].at[at], v_send.at[it], v_recv.at[it, k], rep=rep_of(dx, dyh, dc))

        def send_scales(_):
            diagonal = lax.broadcasted_iota(jnp.int32, (BLK, BLK), 0) == lax.broadcasted_iota(jnp.int32, (BLK, BLK), 1)
            for h in range(2):
                at = pl.ds(h * BLK, BLK)
                mean = jnp.sum(squares[0, at] + squares[1, at], axis=-1, keepdims=True) / C
                scale = lax.rsqrt(mean + 1e-6)
                if nxt is None:
                    for n in range(2):
                        out[at, n * HALF : (n + 1) * HALF] = (kept[n, at] * scale).astype(BF16)
                else:
                    scales[it][0, pl.ds(h, 1)] = jnp.sum(jnp.where(diagonal, scale, 0.0), axis=0, keepdims=True)
            if nxt is not None:
                for k in range(N_REP - 1):
                    v_copy(k).start()

        def take_scales(_):
            for k in range(N_REP - 1):
                v_copy(k).wait_recv()

        def take_shares(n):
            for q in range(NQ):
                if n_of(q) == n:
                    for k in range(chunks[q][3]):
                        s_copy(k, q).wait_recv()

        return dict(
            m=functools.partial(products, (2,)), n=functools.partial(products, (1, 3)), o=functools.partial(products, (0,)),
            F=far, N=near, C=combine, A=across, Y=across_first, W=around, E=finish,
            P=spread_partner, L=spread_left, M=spread_right, K=share_left, R=share_right, S=share_far,
            V=send_scales, U=take_scales, X=take_shares,
        )

    steps = [steps_of(it) for it in range(ITERS)]
    for step, it, q in ORDER:
        steps[it][step](q)

    remote(lab_all.at[pl.ds(1, N_REP - 1)], lab_all.at[pl.ds(1, N_REP - 1)], lab_send, lab_recv.at[0], rep=twin).wait_send()
    for it in range(ITERS):
        sent = ps[it].at[:, pl.ds(0, 7)]
        remote(sent, sent, z_send.at[it], y_recv.at[it, 0], team=beside).wait_send()
        if it + 1 < ITERS:
            sent = zin.at[:, :, pl.ds(0, 5)]
            remote(sent, sent, g_send.at[it], g_recv.at[it, 0, 0], rep=twin).wait_send()
            sent = scales[it].at[pl.ds(1, N_REP - 1)]
            remote(sent, sent, v_send.at[it], v_recv.at[it, 0], rep=twin).wait_send()


def on_device(affinity, col_index, labels):
    vmem = pl.BlockSpec(memory_space=pltpu.VMEM)
    dma = pltpu.SemaphoreType.DMA
    scores = pltpu.VMEM((8, 2, 2, BLK, HALF), BF16)
    partials = pltpu.VMEM((2, 8, ROWS, HALF), BF16)
    return pl.pallas_call(
        kernel,
        out_shape=jax.ShapeDtypeStruct((ROWS, C), BF16),
        in_specs=[pl.BlockSpec(memory_space=pl.ANY), pl.BlockSpec(memory_space=pltpu.SMEM), vmem],
        out_specs=vmem,
        scratch_shapes=[
            pltpu.VMEM((16, KB, BLK, BLK), BF16),
            pltpu.VMEM((8, 2, KB, BLK, BLK), BF16),
            pltpu.VMEM((N_REP, 2, BLK), jnp.int32),
            scores, scores, scores, scores, scores, scores,
            partials, partials, partials,
            pltpu.VMEM((ITERS, 2, 6, ROWS, HALF), BF16),
            pltpu.VMEM((ITERS, 2, ROWS, HALF), BF16),
            pltpu.VMEM((ITERS, 2, 2, ROWS, HALF), BF16),
            pltpu.VMEM((ITERS, 2, ROWS, HALF), BF16),
            pltpu.VMEM((ITERS, 2, 4, ROWS, HALF), BF16),
            pltpu.VMEM((ITERS, 2, 4, ROWS, HALF), BF16),
            pltpu.VMEM((2, ROWS, HALF // 2), F32),
            pltpu.VMEM((2, ROWS, HALF), F32),
            pltpu.VMEM((N_REP, 2, BLK), F32), pltpu.VMEM((N_REP, 2, BLK), F32),
            dma,
            dma, dma((N_REP - 1,)),
            dma((ITERS,)), dma((ITERS, NQ, 6)),
            dma((ITERS, NQ)),
            dma((ITERS - 1,)), dma((ITERS - 1, NQ, 7)),
            dma((ITERS - 1, NQ, 4)),
            dma((ITERS - 1,)), dma((ITERS - 1, N_REP - 1)),
        ],
        compiler_params=pltpu.CompilerParams(
            collective_id=0, has_side_effects=True, vmem_limit_bytes=50 * 2**20
        ),
    )(affinity[0], col_index[0].T, labels.reshape(2, BLK))


def solution(mesh):
    in_specs = (P("team", "rep", None, None, None), P("team", "rep", None), P(("rep", "team")))
    out_specs = P(("rep", "team"), None)
    return jax.shard_map(
        on_device, mesh=mesh, in_specs=in_specs, out_specs=out_specs, check_vma=False
    )
```
